128 devices in a mesh: tiles: 64 (over z, y, x), grp: 2 (over core).
Axes of the slice: x: 4, y: 4, z: 4, core: 2. Of those that a mesh axis runs over, the one named last changes fastest.
Arguments:
- strips: bfloat16 [256, 256, 4096], P(('tiles', 'grp'))
- edge_colour: int32 [128, 2], P(('tiles', 'grp')), may hold values from 0 to 1, as said below
- patch_offsets: int32 [128, 2, 16, 2], P(('tiles', 'grp')), may hold values from 0 to 3968, as said below
- patch_live: int32 [128, 2], P(('tiles', 'grp')), may hold values from 4 to 16
- node_ids: int32 [128, 2, 16], P(('tiles', 'grp')), may hold values from 0 to 16383
Outputs:
- node_sums: float32 [2, 16384], P(None, ('tiles', 'grp'))
The draws below stay inside these ranges and needn't reach their ends.
Inputs may be any that keep to these rules, and one draw needn't show every extreme that they name: `edge_colour`: for each device its 2 entries name different strips. `patch_offsets`: A device and the device it is paired with in a round have the same offsets in that round. Rows are at most 128.
All inputs are finite; a program needn't handle non-finite values.
Results may differ from the reference program's by a relative error of at most 0.0003.
Values may be sent and summed in bfloat16 or wider, within the bound.
No kernel may reach another device: no remote copies, remote signals or barrier semaphores. Data moves between devices by JAX's collectives and lax.ppermute only.
A program may use at most 64 MiB of HBM per device.

```python
import math
import jax
import jax.numpy as jnp
from jax import lax

PATCH = 128
STRIP_R = 256
WIDTH = 4096
ROUNDS = 2
PATCH_DEV = 16
NODES = 16384
N_TILES = 64
N_GRP = 2
DEVICES = 128


def device_flips(key):
    return jax.random.randint(jax.random.fold_in(key, 7), (DEVICES,), 0, 2)


def pair_number(device, round_index):
    tile_index = device // N_GRP
    group_index = device % N_GRP
    pair_bit = jnp.where(round_index == 0, 0, N_TILES.bit_length() - 2)
    side = jnp.right_shift(tile_index, pair_bit) % 2
    lower = tile_index - side * jnp.left_shift(1, pair_bit)
    return ((lower * N_GRP + group_index) * ROUNDS + round_index, side)


def draw_edge_colour(key, part):
    flips = device_flips(key)
    rounds = jnp.arange(ROUNDS, dtype=jnp.int32)
    return jnp.bitwise_xor(rounds[None, :], flips[:, None]).astype(jnp.int32)


def draw_patch_offsets(key, part):

    def single(device, round_index):
        number, side = pair_number(device, round_index)
        pair_key = jax.random.fold_in(key, 5000 + number)
        rows = jax.random.randint(jax.random.fold_in(pair_key, 1), (PATCH_DEV,), 0, STRIP_R - PATCH + 1)
        cols = jax.random.randint(jax.random.fold_in(pair_key, 2), (PATCH_DEV,), 0, WIDTH - PATCH + 1)
        rows = rows.at[0].set(0)
        cols = cols.at[0].set(WIDTH - PATCH)
        return jnp.stack([rows, cols], axis=1)
    devices = jnp.arange(DEVICES, dtype=jnp.int32)
    rounds = jnp.arange(ROUNDS, dtype=jnp.int32)
    table = jax.vmap(lambda device: jax.vmap(lambda rnd: single(device, rnd))(rounds))(devices)
    return table.astype(jnp.int32)


def draw_patch_live(key, part):
    counts = jax.random.randint(jax.random.fold_in(key, 11), (DEVICES, ROUNDS), PATCH_DEV // 4, PATCH_DEV + 1)
    return counts.at[0, 0].set(PATCH_DEV).astype(jnp.int32)


def draw_strips(key, part):
    flips = device_flips(key)
    reach = 3 * PATCH // 8
    block_count = WIDTH // PATCH
    row_positions = jnp.arange(STRIP_R, dtype=jnp.int32)
    col_positions = jnp.arange(WIDTH, dtype=jnp.int32)
    block_of_col = col_positions // PATCH

    def single(index):
        device = index // ROUNDS
        strip_index = index % ROUNDS
        round_index = jnp.bitwise_xor(strip_index, flips[device])
        number, side = pair_number(device, round_index)
        base_key = jax.random.fold_in(key, 100000 + number)
        base = jax.random.normal(base_key, (STRIP_R, WIDTH), jnp.float32)
        row_moves = jax.random.randint(jax.random.fold_in(base_key, 1), (block_count,), -reach, reach + 1)
        col_moves = jax.random.randint(jax.random.fold_in(base_key, 2), (block_count,), -reach, reach + 1)
        row_source = (row_positions[:, None] - side * row_moves[block_of_col][None, :]) % STRIP_R
        col_source = (col_positions[None, :] - side * col_moves[block_of_col][None, :]) % WIDTH
        col_source = jnp.broadcast_to(col_source, (STRIP_R, WIDTH))
        moved = base[row_source, col_source]
        noise = jax.random.normal(jax.random.fold_in(jax.random.fold_in(key, 3), index), (STRIP_R, WIDTH), jnp.float32)
        result = moved + 0.5 * noise
        return result
    return lax.map(single, jnp.arange(DEVICES * ROUNDS, dtype=jnp.int32)).astype(jnp.bfloat16)


def set_ends(drawn, key, least, top_value):
    shape = drawn.shape
    index_at = [jax.random.randint(jax.random.fold_in(key, axis), (), 0, shape[axis]) for axis in range(len(shape))]
    drawn = drawn.at[tuple(index_at)].set(least)
    longest = shape.index(max(shape))
    index_at[longest] = (index_at[longest] + 1) % shape[longest]
    return drawn.at[tuple(index_at)].set(top_value)


def setup_inputs(seed: int = 0) -> dict:
    key_of = jax.random.split(jax.random.key(seed), 6)
    return {
        "strips": draw_strips(jax.random.fold_in(key_of[5], 71), 0),
        "edge_colour": draw_edge_colour(jax.random.fold_in(key_of[5], 71), 0),
        "patch_offsets": draw_patch_offsets(jax.random.fold_in(key_of[5], 71), 0),
        "patch_live": draw_patch_live(jax.random.fold_in(key_of[5], 71), 0),
        "node_ids": set_ends(jax.random.randint(key_of[4], (DEVICES, ROUNDS, PATCH_DEV), 0, NODES), jax.random.fold_in(key_of[4], 1), 0, NODES - 1).astype(jnp.int32),
    }


highest = lax.Precision.HIGHEST

def tables(length):
    indices = jnp.arange(length, dtype=jnp.int32)
    product = indices[:, None] * indices[None, :] % length
    angles = product.astype(jnp.float32) * (2.0 * math.pi / length)
    return (jnp.cos(angles), jnp.sin(angles))

def right_mul(patches, matrix):
    return jnp.einsum('pab,bc->pac', patches, matrix, precision=highest)

def left_mul(matrix, patches):
    return jnp.einsum('ab,pbc->pac', matrix, patches, precision=highest)

def forward(patches, cosine, sine):
    real_half = right_mul(patches, cosine)
    imag_half = -right_mul(patches, sine)
    return (left_mul(cosine, real_half) + left_mul(sine, imag_half), left_mul(cosine, imag_half) - left_mul(sine, real_half))

def displacement(first_set, second_set):
    length = first_set.shape[-1]
    cosine, sine = tables(length)
    first_real, first_imag = forward(first_set, cosine, sine)
    second_real, second_imag = forward(second_set, cosine, sine)
    cross_real = first_real * second_real + first_imag * second_imag
    cross_imag = first_imag * second_real - first_real * second_imag
    magnitude = jnp.sqrt(cross_real * cross_real + cross_imag * cross_imag)
    denominator = magnitude + 0.1 * lax.optimization_barrier(jnp.mean(magnitude, axis=(1, 2), keepdims=True)) + 1e-06
    white_real = cross_real / denominator
    white_imag = cross_imag / denominator
    back_real = left_mul(cosine, white_real) - left_mul(sine, white_imag)
    back_imag = left_mul(cosine, white_imag) + left_mul(sine, white_real)
    surface = (right_mul(back_real, cosine) - right_mul(back_imag, sine)) / float(length * length)
    flattened = surface.reshape(surface.shape[0], length * length)
    centre = lax.optimization_barrier(jnp.mean(flattened, axis=1, keepdims=True))
    spread = jnp.sqrt(lax.optimization_barrier(jnp.mean((flattened - centre) * (flattened - centre), axis=1, keepdims=True)) + 1e-06)
    scores = 2.0 * (flattened - centre) / spread
    weights = jax.nn.softmax(scores, axis=-1).reshape(surface.shape)
    coords = ((jnp.arange(length, dtype=jnp.int32) + length // 2) % length - length // 2).astype(jnp.float32)
    coord_scale = float(length // 8)
    row_shift = lax.optimization_barrier(jnp.sum(weights * coords[None, :, None], axis=(1, 2))) / coord_scale
    col_shift = lax.optimization_barrier(jnp.sum(weights * coords[None, None, :], axis=(1, 2))) / coord_scale
    return jnp.stack([row_shift, col_shift])

def window_stack(strip, offsets):

    def single(corner):
        return lax.dynamic_slice(strip, (corner[0], corner[1]), (PATCH, PATCH))
    return jax.vmap(single)(offsets)

def reference(strips, edge_colour, patch_offsets, patch_live, node_ids):
    stacked = strips.reshape(DEVICES, ROUNDS, STRIP_R, WIDTH)

    def one_device(device):
        tile_index = device // N_GRP
        group_index = device % N_GRP
        first_list = []
        second_list = []
        for round_index in range(ROUNDS):
            pair_bit = 0 if round_index == 0 else N_TILES.bit_length() - 2
            partner = ((tile_index ^ 1 << pair_bit) * N_GRP + group_index).astype(jnp.int32)
            own_strip = stacked[device, edge_colour[device, round_index]]
            other_strip = stacked[partner, edge_colour[partner, round_index]]
            corners = patch_offsets[device, round_index]
            first_list.append(window_stack(own_strip, corners))
            second_list.append(window_stack(other_strip, corners))
        first_set = jnp.concatenate(first_list, axis=0).astype(jnp.float32)
        second_set = jnp.concatenate(second_list, axis=0).astype(jnp.float32)
        shifts = displacement(first_set, second_set)
        slot_index = jnp.arange(PATCH_DEV, dtype=jnp.int32)
        live_mask = (slot_index[None, :] < patch_live[device][:, None]).reshape(ROUNDS * PATCH_DEV)
        return jnp.where(live_mask[None, :], shifts, jnp.zeros_like(shifts))
    values = lax.map(one_device, jnp.arange(DEVICES).astype(jnp.int32))
    values = jnp.transpose(values, (0, 2, 1)).reshape(DEVICES * ROUNDS * PATCH_DEV, 2)
    node_list = node_ids.reshape(DEVICES * ROUNDS * PATCH_DEV)
    summed = jax.ops.segment_sum(values, node_list, num_segments=NODES)
    return jnp.transpose(summed)
```

```python
import functools
import math

import jax
import jax.numpy as jnp
import ml_dtypes
import numpy as np
from jax import lax
from jax.experimental import pallas as pl
from jax.experimental.pallas import tpu as pltpu
from jax.sharding import PartitionSpec as P

SIDE = 128
HALF = 8
SLOTS = 16
CELLS = SIDE * SIDE
BITS = (0, 5)

f32 = jnp.float32
bf16 = jnp.bfloat16


def fourier_tables():
    index = np.arange(SIDE)
    angle = (np.outer(index, index) % SIDE) * (2.0 * math.pi / SIDE)
    cosine, sine = np.cos(angle), np.sin(angle)

    def pieces(table):
        high = table.astype(ml_dtypes.bfloat16)
        low = (table - high.astype(np.float64)).astype(ml_dtypes.bfloat16)
        return high, low

    cos_high, cos_low = pieces(cosine)
    sin_high, sin_low = pieces(sine)
    first = np.block([[cos_high, sin_high], [cos_low, sin_low]])
    left_high = np.block([[cos_high, -sin_high], [sin_high, cos_high]])
    left_low = np.block([[cos_low, -sin_low], [sin_low, cos_low]])
    left = np.concatenate([left_high, left_low, left_high], axis=1)
    right = np.concatenate([left_high.T, left_high.T, left_low.T], axis=0)
    return first, left, right


def tile_side(bit):
    return (lax.axis_index("tiles") >> bit) & 1


def cut_kernel(rounds, mine, colour_ref, corner_ref, strips_ref, out_ref, blocks, sems):
    rows = lax.broadcasted_iota(jnp.int32, (SIDE, 2 * SIDE), 0)
    lanes = lax.broadcasted_iota(jnp.int32, (SIDE, SIDE), 1)
    last = strips_ref.shape[2] // SIDE - 2
    plan = []
    for round_index in rounds:
        side = tile_side(BITS[round_index])
        start = HALF * side if mine else HALF - HALF * side
        for j in range(HALF):
            place = (round_index * SLOTS + start + j) * 2
            row = corner_ref[place]
            col = corner_ref[place + 1]
            block = jnp.minimum(col >> 7, last)
            source = strips_ref.at[
                colour_ref[round_index], :, pl.ds(pl.multiple_of(block * SIDE, SIDE), 2 * SIDE)
            ]
            copy = pltpu.make_async_copy(source, blocks.at[len(plan)], sems.at[len(plan)])
            copy.start()
            plan.append((copy, row, col - block * SIDE))
    for i, (copy, row, shift) in enumerate(plan):
        copy.wait()
        top = blocks[i, :SIDE, :].astype(f32)
        bottom = blocks[i, SIDE:, :].astype(f32)
        both = jnp.where(rows >= row, top, bottom)
        window = jnp.where(lanes >= shift, both[:, :SIDE], both[:, SIDE:])
        out_ref[i] = window.astype(bf16)


def cut(rounds, mine, colour, corners, strips):
    count = len(rounds) * HALF
    return pl.pallas_call(
        functools.partial(cut_kernel, rounds, mine),
        out_shape=jax.ShapeDtypeStruct((count, SIDE, SIDE), bf16),
        in_specs=[
            pl.BlockSpec(memory_space=pltpu.SMEM),
            pl.BlockSpec(memory_space=pltpu.SMEM),
            pl.BlockSpec(memory_space=pl.ANY),
        ],
        out_specs=pl.BlockSpec(memory_space=pltpu.VMEM),
        scratch_shapes=[
            pltpu.VMEM((count, 2 * SIDE, 2 * SIDE), bf16),
            pltpu.SemaphoreType.DMA((count,)),
        ],
        compiler_params=pltpu.CompilerParams(vmem_limit_bytes=24 * 1024 * 1024),
        cost_estimate=pl.CostEstimate(
            flops=count * CELLS * 8, bytes_accessed=count * CELLS * 10, transcendentals=0
        ),
    )(colour, corners, strips)


def split(x):
    high = x.astype(bf16)
    return high, (x - high.astype(f32)).astype(bf16)


def matmul(a, b):
    return jnp.dot(a, b, preferred_element_type=f32)


def left_mul(table, x):
    high, low = split(x)
    return matmul(table, jnp.concatenate([high, high, low], axis=0))


def right_mul(x, table):
    high, low = split(x)
    return matmul(jnp.concatenate([high, low, high], axis=1), table)


def forward_pair(first_window, second_window, first, left):
    parts = []
    for window in (first_window, second_window):
        parts.append(matmul(jnp.concatenate([window, window], axis=1), first))
    a, b = parts
    stacked = jnp.concatenate(
        [
            jnp.concatenate([a[:, :SIDE], b[:, :SIDE]], axis=1),
            jnp.concatenate([a[:, SIDE:], b[:, SIDE:]], axis=1),
        ],
        axis=0,
    )
    return left_mul(left, stacked)


def forward_kernel(window_ref, first_ref, left_ref, out_ref):
    for q in range(2):
        out_ref[q] = forward_pair(
            window_ref[2 * q], window_ref[2 * q + 1], first_ref[...], left_ref[...]
        )


def forward(windows, first, left):
    count = windows.shape[0]
    whole = lambda table: pl.BlockSpec(table.shape, lambda i: (0, 0))
    return pl.pallas_call(
        forward_kernel,
        grid=(count // 4,),
        out_shape=jax.ShapeDtypeStruct((count // 2, 2 * SIDE, 2 * SIDE), f32),
        in_specs=[
            pl.BlockSpec((4, SIDE, SIDE), lambda i: (i, 0, 0)),
            whole(first),
            whole(left),
        ],
        out_specs=pl.BlockSpec((2, 2 * SIDE, 2 * SIDE), lambda i: (i, 0, 0)),
        cost_estimate=pl.CostEstimate(
            flops=count * 8 * 2 * SIDE**3 * 2, bytes_accessed=count * CELLS * 10, transcendentals=0
        ),
    )(windows, first, left)


def total(x):
    return jnp.sum(jnp.sum(x, axis=0, keepdims=True), axis=1, keepdims=True)


def correlate_kernel(
    ids_ref, near_ref, window_ref, first_ref, left_ref, right_ref, out_ref, plain, ramp, edge
):
    step = pl.program_id(0)
    spectra = []
    for q in range(2):
        near = near_ref[q]
        far = forward_pair(
            window_ref[2 * q], window_ref[2 * q + 1], first_ref[...], left_ref[...]
        )
        near_real, near_imag = near[:SIDE], near[SIDE:]
        far_real, far_imag = far[:SIDE], far[SIDE:]
        cross_real = near_real * far_real + near_imag * far_imag
        cross_imag = near_real * far_imag - near_imag * far_real
        square = cross_real * cross_real + cross_imag * cross_imag
        magnitude = jnp.sqrt(square)
        whites = []
        for h in range(2):
            part = slice(h * SIDE, (h + 1) * SIDE)
            size = magnitude[:, part]
            scale = 1.0 / (size + (total(size) * (0.1 / CELLS) + 1e-6))
            whites.append((cross_real[:, part] * scale, cross_imag[:, part] * scale))
        (a_real, a_imag), (b_real, b_imag) = whites
        spectra.append((a_real - b_imag, a_imag + b_real))
    stacked = jnp.concatenate(
        [
            jnp.concatenate([spectra[0][0], spectra[1][0]], axis=1),
            jnp.concatenate([spectra[0][1], spectra[1][1]], axis=1),
        ],
        axis=0,
    )
    back = left_mul(left_ref[...], stacked)
    rows = jnp.concatenate(
        [
            jnp.concatenate([back[:SIDE, :SIDE], back[SIDE:, :SIDE]], axis=1),
            jnp.concatenate([back[:SIDE, SIDE:], back[SIDE:, SIDE:]], axis=1),
        ],
        axis=0,
    )
    surfaces = right_mul(rows, right_ref[...])
    row_index = lax.broadcasted_iota(jnp.int32, (SIDE, SIDE), 0)
    row_coord = (((row_index + SIDE // 2) & (SIDE - 1)) - SIDE // 2).astype(f32)
    for p in range(4):
        q, h = divmod(p, 2)
        surface = surfaces[q * SIDE : (q + 1) * SIDE, h * SIDE : (h + 1) * SIDE]
        mean = total(surface) * (1.0 / CELLS)
        variance = total(surface * surface) * (1.0 / CELLS) - mean * mean
        peak = jnp.max(jnp.max(surface, axis=0, keepdims=True), axis=1, keepdims=True)
        spread = jnp.sqrt(jnp.maximum(variance, 0.0) * (1.0 / CELLS**2) + 1e-6)
        factor = (2.0 / CELLS) / spread
        weight = jnp.exp((surface - peak) * factor)
        place = pl.ds(step * 4 + p, 1)
        plain[place, :] = jnp.sum(weight, axis=0, keepdims=True)
        ramp[place, :] = jnp.sum(weight * row_coord, axis=0, keepdims=True)
        edge[place, :] = weight[SIDE // 2 : SIDE // 2 + 1, :]

    @pl.when(step == pl.num_programs(0) - 1)
    def finish():
        lane = lax.broadcasted_iota(jnp.int32, (8, SIDE), 1)
        sublane = lax.broadcasted_iota(jnp.int32, (8, SIDE), 0)
        coord = (((lane + SIDE // 2) & (SIDE - 1)) - SIDE // 2).astype(f32)
        chosen = jnp.where(lane == SIDE // 2, 1.0, 0.0)
        query = jnp.where(sublane == 0, 1.0, jnp.where(sublane == 1, coord, chosen))

        def reduce(ref):
            return lax.dot_general(
                query,
                ref[...],
                (((1,), (1,)), ((), ())),
                precision=lax.Precision.HIGHEST,
                preferred_element_type=f32,
            )

        plain_sums, ramp_sums, edge_sums = reduce(plain), reduce(ramp), reduce(edge)
        inverse = 1.0 / plain_sums[0:1]
        scale = 8.0 / SIDE
        row_shift = ramp_sums[0:1] * inverse * scale
        col_shift = plain_sums[1:2] * inverse * scale
        row_other = -row_shift - edge_sums[0:1] * inverse * (SIDE * scale)
        col_other = -col_shift - plain_sums[2:3] * inverse * (SIDE * scale)
        out = ids_ref[...]
        lane = lax.broadcasted_iota(jnp.int32, (1, SIDE), 1)
        for i, value in enumerate((row_shift, col_shift, row_other, col_other)):
            moved = jnp.concatenate(
                [jnp.zeros((1, 32 + 16 * i), f32), value, jnp.zeros((1, 80 - 16 * i), f32)], axis=1
            )
            inside = (lane >= 32 + 16 * i) & (lane < 48 + 16 * i)
            out = jnp.where(inside, moved, out)
        out_ref[...] = out


def correlate(ids, near, windows, first, left, right):
    count = windows.shape[0]
    whole = lambda table: pl.BlockSpec(table.shape, lambda i: (0, 0))
    return pl.pallas_call(
        correlate_kernel,
        grid=(count // 4,),
        out_shape=jax.ShapeDtypeStruct((1, SIDE), f32),
        in_specs=[
            whole(ids),
            pl.BlockSpec((2, 2 * SIDE, 2 * SIDE), lambda i: (i, 0, 0)),
            pl.BlockSpec((4, SIDE, SIDE), lambda i: (i, 0, 0)),
            whole(first),
            whole(left),
            whole(right),
        ],
        out_specs=pl.BlockSpec((1, SIDE), lambda i: (0, 0)),
        scratch_shapes=[pltpu.VMEM((count, SIDE), f32)] * 3,
        cost_estimate=pl.CostEstimate(
            flops=count * 12 * 2 * SIDE**3 * 2,
            bytes_accessed=count * CELLS * 10,
            transcendentals=count * CELLS * 3,
        ),
    )(ids, near, windows, first, left, right)


def collect_kernel(packed_ref, out_ref):
    packed = packed_ref[...].T
    base = (lax.axis_index("tiles") * lax.axis_size("grp") + lax.axis_index("grp")) * SIDE
    device = lax.broadcasted_iota(jnp.int32, (HALF, SIDE), 1)
    node = lax.broadcasted_iota(jnp.int32, (SIDE, SIDE), 0).astype(f32)
    sums = [jnp.zeros((SIDE, SIDE), f32), jnp.zeros((SIDE, SIDE), f32)]
    for r, bit in enumerate(BITS):
        reach = 2 << bit
        side = (device >> (bit + 1)) & 1
        own, other = [], []
        for c in range(2):
            own.append(packed[32 + 16 * c + HALF * r :][:HALF])
            far = packed[64 + 16 * c + HALF * r :][:HALF]
            up = pltpu.roll(far, SIDE - reach, 1)
            down = pltpu.roll(far, reach, 1)
            other.append(jnp.where(side == 0, up, down))
        for h in range(2):
            local = packed[SLOTS * r + HALF * h :][:HALF] - base.astype(f32)
            values = [jnp.where(side == h, own[c], other[c]) for c in range(2)]
            for j in range(HALF):
                hit = node == local[j : j + 1]
                for c in range(2):
                    sums[c] = sums[c] + jnp.where(hit, values[c][j : j + 1], 0.0)
    ones = jnp.ones((8, SIDE), f32)
    for c in range(2):
        summed = lax.dot_general(
            ones,
            sums[c],
            (((1,), (1,)), ((), ())),
            precision=lax.Precision.HIGHEST,
            preferred_element_type=f32,
        )
        out_ref[c : c + 1] = summed[0:1]


def collect(packed):
    return pl.pallas_call(
        collect_kernel,
        out_shape=jax.ShapeDtypeStruct((2, SIDE), f32),
        in_specs=[pl.BlockSpec(memory_space=pltpu.VMEM)],
        out_specs=pl.BlockSpec(memory_space=pltpu.VMEM),
    )(packed)


def swap(x, bit):
    pairs = [(i, i ^ (1 << bit)) for i in range(lax.axis_size("tiles"))]
    return lax.ppermute(x, "tiles", pairs)


def on_device(strips, edge_colour, patch_offsets, patch_live, node_ids):
    first, left, right = (jnp.asarray(table) for table in fourier_tables())
    colour = edge_colour.reshape(2)
    corners = patch_offsets.reshape(4 * SLOTS)
    far_late = swap(cut((1,), False, colour, corners, strips), BITS[1])
    far_early = swap(cut((0,), False, colour, corners, strips), BITS[0])
    near = forward(cut((0, 1), True, colour, corners, strips), first, left)
    slot = jnp.arange(SLOTS, dtype=jnp.int32)
    live = slot[None, :] < patch_live[0][:, None]
    ids = jnp.where(live, node_ids[0], -1).astype(f32).reshape(1, 2 * SLOTS)
    ids = jnp.pad(ids, ((0, 0), (0, SIDE - 2 * SLOTS)))
    far = jnp.concatenate([far_early, far_late], axis=0)
    packed = correlate(ids, near, far, first, left, right)
    spread = jnp.broadcast_to(packed, (SIDE, SIDE))
    gathered = lax.all_to_all(spread, ("tiles", "grp"), 0, 0, tiled=True)
    return collect(gathered)


def solution(mesh):
    placed = (
        P(("tiles", "grp"), None, None),
        P(("tiles", "grp"), None),
        P(("tiles", "grp"), None, None, None),
        P(("tiles", "grp"), None),
        P(("tiles", "grp"), None, None),
    )
    return jax.shard_map(
        on_device, mesh=mesh, in_specs=placed, out_specs=P(None, ("tiles", "grp")), check_vma=False
    )
```

```python
import functools
import math

import jax
import jax.numpy as jnp
import ml_dtypes
import numpy as np
from jax import lax
from jax.experimental import pallas as pl
from jax.experimental.pallas import tpu as pltpu
from jax.sharding import PartitionSpec as P

SIDE = 128
HALF = 8
SLOTS = 16
ROWS = 64
CUT_LIMIT = 16
CELLS = SIDE * SIDE
BITS = (0, 5)

f32 = jnp.float32
bf16 = jnp.bfloat16


def fourier_tables():
    index = np.arange(SIDE)
    angle = (np.outer(index, index) % SIDE) * (2.0 * math.pi / SIDE)
    cosine, sine = np.cos(angle), np.sin(angle)

    def pieces(table):
        high = table.astype(ml_dtypes.bfloat16)
        low = (table - high.astype(np.float64)).astype(ml_dtypes.bfloat16)
        return high, low

    cos_high, cos_low = pieces(cosine)
    sin_high, sin_low = pieces(sine)
    first = np.block([[cos_high, sin_high], [cos_low, sin_low]])
    left_high = np.block([[cos_high, -sin_high], [sin_high, cos_high]])
    left_low = np.block([[cos_low, -sin_low], [sin_low, cos_low]])
    left = np.concatenate([left_high, left_low, left_high], axis=1)
    right = np.concatenate([left_high.T, left_high.T, left_low.T], axis=0)
    return first, left, right


def tile_side(bit):
    return (lax.axis_index("tiles") >> bit) & 1


def cut_kernel(
    colour_ref, corner_ref, strips_ref, send_early, send_late, own_early, own_late, held, sems
):
    count = held.shape[1] // ROWS
    plans = []
    for r in range(2):
        plan = []
        for i in range(count):
            rows = pl.ds(i * ROWS, ROWS)
            copy = pltpu.make_async_copy(
                strips_ref.at[colour_ref[0, r], rows], held.at[r, rows], sems.at[r, i]
            )
            copy.start()
            plan.append(copy)
        plans.append(plan)
    last = held.shape[2] // SIDE - 1
    rows = lax.broadcasted_iota(jnp.int32, (SIDE, SIDE), 0)
    lanes = lax.broadcasted_iota(jnp.int32, (SIDE, SIDE), 1)
    for r, outs in enumerate(((send_early, own_early), (send_late, own_late))):
        for copy in plans[r]:
            copy.wait()
        side = tile_side(BITS[r])
        for out_ref, start in zip(outs, (HALF - HALF * side, HALF * side)):
            for j in range(HALF):
                row = corner_ref[0, r, 0, start + j]
                col = corner_ref[0, r, 1, start + j]
                block = col >> 7
                shift = col - block * SIDE
                halves = []
                for b in (block, jnp.minimum(block + 1, last)):
                    at = pl.ds(pl.multiple_of(b * SIDE, SIDE), SIDE)
                    top = held[r, :SIDE, at].astype(f32)
                    bottom = held[r, SIDE:, at].astype(f32)
                    halves.append(jnp.where(rows >= row, top, bottom))
                out_ref[j] = jnp.where(lanes >= shift, *halves).astype(bf16)


scalars = pl.BlockSpec(memory_space=pltpu.SMEM)
vectors = pl.BlockSpec(memory_space=pltpu.VMEM)
far_memory = pl.BlockSpec(memory_space=pltpu.HBM)


def cut(colour, corners, strips):
    windows = jax.ShapeDtypeStruct((HALF, SIDE, SIDE), bf16)
    return pl.pallas_call(
        cut_kernel,
        out_shape=(windows,) * 4,
        in_specs=[scalars, scalars, far_memory],
        out_specs=(vectors,) * 4,
        scratch_shapes=[
            pltpu.VMEM(strips.shape, bf16),
            pltpu.SemaphoreType.DMA((2, strips.shape[1] // ROWS)),
        ],
        compiler_params=pltpu.CompilerParams(vmem_limit_bytes=CUT_LIMIT * 1024 * 1024),
        cost_estimate=pl.CostEstimate(
            flops=4 * HALF * CELLS * 8, bytes_accessed=4 * HALF * CELLS * 10, transcendentals=0
        ),
    )(colour, corners, strips)


def split(x):
    high = x.astype(bf16)
    return high, (x - high.astype(f32)).astype(bf16)


def matmul(a, b):
    return jnp.dot(a, b, preferred_element_type=f32)


def left_mul(table, x):
    high, low = split(x)
    return matmul(table, jnp.concatenate([high, high, low], axis=0))


def right_mul(x, table):
    high, low = split(x)
    return matmul(jnp.concatenate([high, low, high], axis=1), table)


def forward_pair(first_window, second_window, first, left):
    parts = []
    for window in (first_window, second_window):
        parts.append(matmul(jnp.concatenate([window, window], axis=1), first))
    a, b = parts
    stacked = jnp.concatenate(
        [
            jnp.concatenate([a[:, :SIDE], b[:, :SIDE]], axis=1),
            jnp.concatenate([a[:, SIDE:], b[:, SIDE:]], axis=1),
        ],
        axis=0,
    )
    return left_mul(left, stacked)


def near_kernel(own_early, own_late, first_ref, left_ref, early_ref, late_ref):
    for window_ref, out_ref in ((own_early, early_ref), (own_late, late_ref)):
        for q in range(HALF // 2):
            out_ref[q] = forward_pair(
                window_ref[2 * q], window_ref[2 * q + 1], first_ref[...], left_ref[...]
            )


def near_spectra(own_early, own_late, first, left):
    shape = jax.ShapeDtypeStruct((HALF // 2, 2 * SIDE, 2 * SIDE), f32)
    return pl.pallas_call(
        near_kernel,
        out_shape=(shape, shape),
        in_specs=[vectors] * 4,
        out_specs=(vectors, vectors),
        compiler_params=pltpu.CompilerParams(vmem_limit_bytes=32 * 1024 * 1024),
        cost_estimate=pl.CostEstimate(
            flops=SLOTS * 8 * 2 * SIDE**3 * 2, bytes_accessed=SLOTS * CELLS * 10, transcendentals=0
        ),
    )(own_early, own_late, first, left)


def total(x):
    return jnp.sum(jnp.sum(x, axis=0, keepdims=True), axis=1, keepdims=True)


def correlate_group(near, windows, first_ref, left_ref, right_ref, place, plain, ramp, edge):
    spectra = []
    for q in range(2):
        here = near[q]
        far = forward_pair(windows[2 * q], windows[2 * q + 1], first_ref[...], left_ref[...])
        near_real, near_imag = here[:SIDE], here[SIDE:]
        far_real, far_imag = far[:SIDE], far[SIDE:]
        cross_real = near_real * far_real + near_imag * far_imag
        cross_imag = near_real * far_imag - near_imag * far_real
        square = cross_real * cross_real + cross_imag * cross_imag
        magnitude = jnp.sqrt(square)
        whites = []
        for h in range(2):
            part = slice(h * SIDE, (h + 1) * SIDE)
            size = magnitude[:, part]
            scale = 1.0 / (size + (total(size) * (0.1 / CELLS) + 1e-6))
            whites.append((cross_real[:, part] * scale, cross_imag[:, part] * scale))
        (a_real, a_imag), (b_real, b_imag) = whites
        spectra.append((a_real - b_imag, a_imag + b_real))
    stacked = jnp.concatenate(
        [
            jnp.concatenate([spectra[0][0], spectra[1][0]], axis=1),
            jnp.concatenate([spectra[0][1], spectra[1][1]], axis=1),
        ],
        axis=0,
    )
    back = left_mul(left_ref[...], stacked)
    rows = jnp.concatenate(
        [
            jnp.concatenate([back[:SIDE, :SIDE], back[SIDE:, :SIDE]], axis=1),
            jnp.concatenate([back[:SIDE, SIDE:], back[SIDE:, SIDE:]], axis=1),
        ],
        axis=0,
    )
    surfaces = right_mul(rows, right_ref[...])
    row_index = lax.broadcasted_iota(jnp.int32, (SIDE, SIDE), 0)
    row_coord = (((row_index + SIDE // 2) & (SIDE - 1)) - SIDE // 2).astype(f32)
    for p in range(4):
        q, h = divmod(p, 2)
        surface = surfaces[q * SIDE : (q + 1) * SIDE, h * SIDE : (h + 1) * SIDE]
        mean = total(surface) * (1.0 / CELLS)
        variance = total(surface * surface) * (1.0 / CELLS) - mean * mean
        peak = jnp.max(jnp.max(surface, axis=0, keepdims=True), axis=1, keepdims=True)
        spread = jnp.sqrt(jnp.maximum(variance, 0.0) * (1.0 / CELLS**2) + 1e-6)
        factor = (2.0 / CELLS) / spread
        weight = jnp.exp((surface - peak) * factor)
        at = slice(place + p, place + p + 1)
        plain[at, :] = jnp.sum(weight, axis=0, keepdims=True)
        ramp[at, :] = jnp.sum(weight * row_coord, axis=0, keepdims=True)
        edge[at, :] = weight[SIDE // 2 : SIDE // 2 + 1, :]


def correlate_groups(near_ref, window_ref, tables, sums):
    for g in range(HALF // 4):
        near = [near_ref[2 * g + q] for q in range(2)]
        windows = [window_ref[4 * g + p] for p in range(4)]
        correlate_group(near, windows, *tables, 4 * g, *sums)


def early_kernel(near_ref, window_ref, first_ref, left_ref, right_ref, out_ref):
    sums = [out_ref.at[i] for i in range(3)]
    correlate_groups(near_ref, window_ref, (first_ref, left_ref, right_ref), sums)


def late_kernel(
    live_ref, ids_ref, early_ref, near_ref, window_ref, first_ref, left_ref, right_ref, out_ref, late
):
    sums = [late.at[i] for i in range(3)]
    correlate_groups(near_ref, window_ref, (first_ref, left_ref, right_ref), sums)
    lane = lax.broadcasted_iota(jnp.int32, (8, SIDE), 1)
    sublane = lax.broadcasted_iota(jnp.int32, (8, SIDE), 0)
    coord = (((lane + SIDE // 2) & (SIDE - 1)) - SIDE // 2).astype(f32)
    chosen = jnp.where(lane == SIDE // 2, 1.0, 0.0)
    query = jnp.where(sublane == 0, 1.0, jnp.where(sublane == 1, coord, chosen))

    def reduce(i):
        both = jnp.concatenate([early_ref[i], late[i]], axis=0)
        return lax.dot_general(
            query,
            both,
            (((1,), (1,)), ((), ())),
            precision=lax.Precision.HIGHEST,
            preferred_element_type=f32,
        )

    plain_sums, ramp_sums, edge_sums = (reduce(i) for i in range(3))
    inverse = 1.0 / plain_sums[0:1]
    scale = 8.0 / SIDE
    row_shift = ramp_sums[0:1] * inverse * scale
    col_shift = plain_sums[1:2] * inverse * scale
    row_other = -row_shift - edge_sums[0:1] * inverse * (SIDE * scale)
    col_other = -col_shift - plain_sums[2:3] * inverse * (SIDE * scale)
    slot = lax.broadcasted_iota(jnp.int32, (1, SLOTS), 1)
    pieces = []
    for r in range(2):
        ids = jnp.where(slot < live_ref[0, r], ids_ref[0, r : r + 1, :], -1)
        pieces.append(ids.astype(f32))
    pieces += [row_shift, col_shift, row_other, col_other]
    pieces.append(jnp.zeros((1, SIDE - 6 * SLOTS), f32))
    row = jnp.concatenate(pieces, axis=1)
    out_ref[...] = jnp.broadcast_to(row, (SIDE, SIDE))


def correlate_cost(count):
    return pl.CostEstimate(
        flops=count * 12 * 2 * SIDE**3 * 2,
        bytes_accessed=count * CELLS * 10,
        transcendentals=count * CELLS * 3,
    )


def correlate_early(near, windows, tables):
    return pl.pallas_call(
        early_kernel,
        out_shape=jax.ShapeDtypeStruct((3, HALF, SIDE), f32),
        in_specs=[vectors] * 5,
        out_specs=vectors,
        compiler_params=pltpu.CompilerParams(vmem_limit_bytes=32 * 1024 * 1024),
        cost_estimate=correlate_cost(HALF),
    )(near, windows, *tables)


def correlate_late(live, ids, early, near, windows, tables):
    return pl.pallas_call(
        late_kernel,
        out_shape=jax.ShapeDtypeStruct((SIDE, SIDE), f32),
        in_specs=[scalars] + [vectors] * 7,
        out_specs=vectors,
        scratch_shapes=[pltpu.VMEM((3, HALF, SIDE), f32)],
        compiler_params=pltpu.CompilerParams(vmem_limit_bytes=32 * 1024 * 1024),
        cost_estimate=correlate_cost(HALF),
    )(live, ids, early, near, windows, *tables)


def collect_kernel(packed_ref, out_ref):
    packed = packed_ref[...].T
    base = (lax.axis_index("tiles") * lax.axis_size("grp") + lax.axis_index("grp")) * SIDE
    device = lax.broadcasted_iota(jnp.int32, (HALF, SIDE), 1)
    node = lax.broadcasted_iota(jnp.int32, (SIDE, SIDE), 0).astype(f32)
    sums = [jnp.zeros((SIDE, SIDE), f32), jnp.zeros((SIDE, SIDE), f32)]
    for r, bit in enumerate(BITS):
        reach = 2 << bit
        side = (device >> (bit + 1)) & 1
        own, other = [], []
        for c in range(2):
            own.append(packed[32 + 16 * c + HALF * r :][:HALF])
            far = packed[64 + 16 * c + HALF * r :][:HALF]
            up = pltpu.roll(far, SIDE - reach, 1)
            down = pltpu.roll(far, reach, 1)
            other.append(jnp.where(side == 0, up, down))
        for h in range(2):
            local = packed[SLOTS * r + HALF * h :][:HALF] - base.astype(f32)
            values = [jnp.where(side == h, own[c], other[c]) for c in range(2)]
            for j in range(HALF):
                hit = node == local[j : j + 1]
                for c in range(2):
                    sums[c] = sums[c] + jnp.where(hit, values[c][j : j + 1], 0.0)
    ones = jnp.ones((8, SIDE), f32)
    for c in range(2):
        summed = lax.dot_general(
            ones,
            sums[c],
            (((1,), (1,)), ((), ())),
            precision=lax.Precision.HIGHEST,
            preferred_element_type=f32,
        )
        out_ref[c : c + 1] = summed[0:1]


def collect(packed):
    return pl.pallas_call(
        collect_kernel,
        out_shape=jax.ShapeDtypeStruct((2, SIDE), f32),
        in_specs=[pl.BlockSpec(memory_space=pltpu.VMEM)],
        out_specs=pl.BlockSpec(memory_space=pltpu.VMEM),
    )(packed)


def swap(x, bit):
    pairs = [(i, i ^ (1 << bit)) for i in range(lax.axis_size("tiles"))]
    return lax.ppermute(x, "tiles", pairs)


def on_device(strips, edge_colour, patch_offsets, patch_live, node_ids):
    tables = [jnp.asarray(table) for table in fourier_tables()]
    corners = jnp.transpose(patch_offsets, (0, 1, 3, 2))
    strips = pltpu.with_memory_space_constraint(strips, pltpu.HBM)
    send_early, send_late, own_early, own_late = cut(edge_colour, corners, strips)
    far_early = swap(send_early, BITS[0])
    far_late = swap(send_late, BITS[1])
    near_early, near_late = near_spectra(own_early, own_late, *tables[:2])
    early = correlate_early(near_early, far_early, tables)
    packed = correlate_late(patch_live, node_ids, early, near_late, far_late, tables)
    packed = packed.reshape(SIDE, 1, SIDE)
    gathered = lax.all_to_all(packed, ("tiles", "grp"), 0, 0, tiled=True)
    return collect(gathered.reshape(SIDE, SIDE))


def solution(mesh):
    placed = (
        P(("tiles", "grp"), None, None),
        P(("tiles", "grp"), None),
        P(("tiles", "grp"), None, None, None),
        P(("tiles", "grp"), None),
        P(("tiles", "grp"), None, None),
    )
    return jax.shard_map(
        on_device, mesh=mesh, in_specs=placed, out_specs=P(None, ("tiles", "grp")), check_vma=False
    )
```

```python
import functools
import math

import jax
import jax.numpy as jnp
import ml_dtypes
import numpy as np
from jax import lax
from jax.experimental import pallas as pl
from jax.experimental.pallas import tpu as pltpu
from jax.sharding import PartitionSpec as P

SIDE = 128
HALF = 8
SLOTS = 16
ROWS = 64
CELLS = SIDE * SIDE
BITS = (0, 5)

f32 = jnp.float32
bf16 = jnp.bfloat16


def fourier_tables():
    index = np.arange(SIDE)
    angle = (np.outer(index, index) % SIDE) * (2.0 * math.pi / SIDE)
    cosine, sine = np.cos(angle), np.sin(angle)

    def pieces(table):
        high = table.astype(ml_dtypes.bfloat16)
        low = (table - high.astype(np.float64)).astype(ml_dtypes.bfloat16)
        return high, low

    cos_high, cos_low = pieces(cosine)
    sin_high, sin_low = pieces(sine)
    first = np.block([[cos_high, sin_high], [cos_low, sin_low]])
    left_high = np.block([[cos_high, -sin_high], [sin_high, cos_high]])
    left_low = np.block([[cos_low, -sin_low], [sin_low, cos_low]])
    second = np.concatenate([left_high.T, left_high.T, left_low.T], axis=0)
    return first, second


def tile_side(bit):
    return (lax.axis_index("tiles") >> bit) & 1


def cut_windows(r, mine, colour_ref, corner_ref, held_ref):
    last = held_ref.shape[2] // SIDE - 1
    rows = lax.broadcasted_iota(jnp.int32, (SIDE, SIDE), 0)
    lanes = lax.broadcasted_iota(jnp.int32, (SIDE, SIDE), 1)
    colour = colour_ref[0, r]
    side = tile_side(BITS[r])
    start = HALF * side if mine else HALF - HALF * side
    for j in range(HALF):
        row = corner_ref[0, r, 0, start + j]
        col = corner_ref[0, r, 1, start + j]
        block = col >> 7
        shift = col - block * SIDE
        halves = []
        for b in (block, jnp.minimum(block + 1, last)):
            at = pl.ds(pl.multiple_of(b * SIDE, SIDE), SIDE)
            top = held_ref[colour, :SIDE, at].astype(f32)
            bottom = held_ref[colour, SIDE:, at].astype(f32)
            halves.append(jnp.where(rows >= row, top, bottom))
        yield jnp.where(lanes >= shift, *halves).astype(bf16)


def hold_kernel(
    colour_hbm, corner_hbm, strips_ref, held_ref, send_ref, colour_ref, corner_ref, sems, small_sems
):
    small = [
        pltpu.make_async_copy(colour_hbm, colour_ref, small_sems.at[0]),
        pltpu.make_async_copy(corner_hbm, corner_ref, small_sems.at[1]),
    ]
    large = []
    for i in range(strips_ref.shape[0]):
        for j in range(strips_ref.shape[1] // ROWS):
            rows = pl.ds(j * ROWS, ROWS)
            large.append(
                pltpu.make_async_copy(strips_ref.at[i, rows], held_ref.at[i, rows], sems.at[i, j])
            )
    for copy in small + large:
        copy.start()
    for copy in small + large:
        copy.wait()
    for j, window in enumerate(cut_windows(0, False, colour_ref, corner_ref, held_ref)):
        send_ref[j] = window


def send_kernel(colour_ref, corner_ref, held_ref, send_ref):
    for j, window in enumerate(cut_windows(1, False, colour_ref, corner_ref, held_ref)):
        send_ref[j] = window


scalars = pl.BlockSpec(memory_space=pltpu.SMEM)
vectors = pl.BlockSpec(memory_space=pltpu.VMEM)
far_memory = pl.BlockSpec(memory_space=pltpu.HBM)


def cut_cost(bytes_accessed):
    return pl.CostEstimate(
        flops=HALF * CELLS * 8, bytes_accessed=bytes_accessed, transcendentals=0
    )


def hold(colour, corners, strips):
    return pl.pallas_call(
        hold_kernel,
        out_shape=(
            jax.ShapeDtypeStruct(strips.shape, bf16),
            jax.ShapeDtypeStruct((HALF, SIDE, SIDE), bf16),
        ),
        in_specs=[far_memory] * 3,
        out_specs=(vectors, vectors),
        scratch_shapes=[
            pltpu.SMEM(colour.shape, jnp.int32),
            pltpu.SMEM(corners.shape, jnp.int32),
            pltpu.SemaphoreType.DMA((2, strips.shape[1] // ROWS)),
            pltpu.SemaphoreType.DMA((2,)),
        ],
        compiler_params=pltpu.CompilerParams(vmem_limit_bytes=16 * 1024 * 1024),
        cost_estimate=cut_cost(2 * strips.size),
    )(*(pltpu.with_memory_space_constraint(x, pltpu.HBM) for x in (colour, corners, strips)))


def cut_late(colour, corners, held):
    return pl.pallas_call(
        send_kernel,
        out_shape=jax.ShapeDtypeStruct((HALF, SIDE, SIDE), bf16),
        in_specs=[scalars, scalars, vectors],
        out_specs=vectors,
        compiler_params=pltpu.CompilerParams(vmem_limit_bytes=16 * 1024 * 1024),
        cost_estimate=cut_cost(HALF * CELLS * 2),
    )(colour, corners, held)


def split(x):
    high = x.astype(bf16)
    return high, (x - high.astype(f32)).astype(bf16)


def matmul(a, b):
    return jnp.dot(a, b, preferred_element_type=f32)


def second_mul(high, low, second):
    return matmul(jnp.concatenate([high, low, high], axis=1), second)


def turned(x):
    blocks = []
    for i in range(x.shape[0] // SIDE):
        rows = x[i * SIDE : (i + 1) * SIDE]
        blocks.append(jnp.concatenate([rows[:, :SIDE].T, rows[:, SIDE:].T], axis=1))
    return jnp.concatenate(blocks, axis=0)


def forward(windows, first, second):
    rows = matmul(jnp.concatenate([windows, windows], axis=1), first)
    high, low = split(rows)
    return second_mul(turned(high), turned(low), second)


def near_kernel(colour_ref, corner_ref, held_ref, first_ref, second_ref, early_ref, late_ref):
    for r, out_ref in enumerate((early_ref, late_ref)):
        windows = jnp.concatenate(
            list(cut_windows(r, True, colour_ref, corner_ref, held_ref)), axis=0
        )
        out_ref[...] = forward(windows, first_ref[...], second_ref[...])


def near_spectra(colour, corners, held, first, second):
    shape = jax.ShapeDtypeStruct((HALF * SIDE, 2 * SIDE), f32)
    return pl.pallas_call(
        near_kernel,
        out_shape=(shape, shape),
        in_specs=[scalars, scalars] + [vectors] * 3,
        out_specs=(vectors, vectors),
        compiler_params=pltpu.CompilerParams(vmem_limit_bytes=32 * 1024 * 1024),
        cost_estimate=pl.CostEstimate(
            flops=SLOTS * 8 * 2 * SIDE**3 * 2, bytes_accessed=SLOTS * CELLS * 10, transcendentals=0
        ),
    )(colour, corners, held, first, second)


def patch_rows(x, p):
    return x[p * SIDE : (p + 1) * SIDE]


def down(x):
    return jnp.sum(x, axis=0, keepdims=True)


def across(rows):
    return jnp.sum(jnp.concatenate(rows, axis=0), axis=1, keepdims=True)


def correlate_group(near_ref, window_ref, first_ref, second_ref, sums_ref):
    far = forward(window_ref[...].reshape(HALF * SIDE, SIDE), first_ref[...], second_ref[...])
    crosses, sizes, size_rows = [], [], []
    for p in range(HALF):
        here, there = near_ref[p * SIDE : (p + 1) * SIDE, :], patch_rows(far, p)
        near_real, near_imag = here[:, :SIDE], here[:, SIDE:]
        far_real, far_imag = there[:, :SIDE], there[:, SIDE:]
        real = near_real * far_real + near_imag * far_imag
        imag = near_real * far_imag - near_imag * far_real
        size = jnp.sqrt(real * real + imag * imag)
        crosses.append((real, imag))
        sizes.append(size)
        size_rows.append(down(size))
    floors = across(size_rows) * (0.1 / CELLS) + 1e-6
    whites = []
    for p in range(HALF):
        scale = 1.0 / (sizes[p] + floors[p : p + 1])
        whites.append((crosses[p][0] * scale, crosses[p][1] * scale))
    spectra = []
    for q in range(HALF // 2):
        (a_real, a_imag), (b_real, b_imag) = whites[2 * q], whites[2 * q + 1]
        spectra.append(jnp.concatenate([a_real - b_imag, a_imag + b_real], axis=1))
    back = second_mul(*split(jnp.concatenate(spectra, axis=0)), second_ref[...])
    high, low = split(back)
    surfaces = second_mul(turned(high), turned(low), second_ref[...])
    patches = []
    for p in range(HALF):
        q, h = divmod(p, 2)
        patches.append(patch_rows(surfaces, q)[:, h * SIDE : (h + 1) * SIDE])
    mean = across([down(x) for x in patches]) * (1.0 / CELLS)
    square = across([down(x * x) for x in patches]) * (1.0 / CELLS)
    peak = jnp.max(
        jnp.concatenate([jnp.max(x, axis=0, keepdims=True) for x in patches], axis=0),
        axis=1,
        keepdims=True,
    )
    variance = jnp.maximum(square - mean * mean, 0.0)
    factor = (2.0 / CELLS) / jnp.sqrt(variance * (1.0 / CELLS**2) + 1e-6)
    row_index = lax.broadcasted_iota(jnp.int32, (SIDE, SIDE), 0)
    row_coord = (((row_index + SIDE // 2) & (SIDE - 1)) - SIDE // 2).astype(f32)
    for p, surface in enumerate(patches):
        weight = jnp.exp((surface - peak[p : p + 1]) * factor[p : p + 1])
        sums_ref[0, p : p + 1, :] = down(weight)
        sums_ref[1, p : p + 1, :] = down(weight * row_coord)
        sums_ref[2, p : p + 1, :] = weight[SIDE // 2 : SIDE // 2 + 1, :]


def late_kernel(
    live_ref, ids_ref, early_ref, near_ref, window_ref, first_ref, second_ref, out_ref, late_ref
):
    correlate_group(near_ref, window_ref, first_ref, second_ref, late_ref)
    lane = lax.broadcasted_iota(jnp.int32, (8, SIDE), 1)
    sublane = lax.broadcasted_iota(jnp.int32, (8, SIDE), 0)
    coord = (((lane + SIDE // 2) & (SIDE - 1)) - SIDE // 2).astype(f32)
    chosen = jnp.where(lane == SIDE // 2, 1.0, 0.0)
    query = jnp.where(sublane == 0, 1.0, jnp.where(sublane == 1, coord, chosen))
    terms = []
    for i in range(3):
        terms += [early_ref[i], late_ref[i]]
    sums = lax.dot_general(
        query,
        jnp.concatenate(terms, axis=0),
        (((1,), (1,)), ((), ())),
        precision=lax.Precision.HIGHEST,
        preferred_element_type=f32,
    )
    slot = lax.broadcasted_iota(jnp.int32, (1, SLOTS), 1)
    pieces = []
    for r in range(2):
        ids = jnp.where(slot < live_ref[0, r], ids_ref[0, r : r + 1, :], -1)
        pieces.append(ids.astype(f32))
    pieces += [sums[0:1], sums[1:2, :SLOTS], sums[2:3, :SLOTS]]
    pieces.append(jnp.zeros((1, SIDE - 7 * SLOTS), f32))
    out_ref[...] = jnp.broadcast_to(jnp.concatenate(pieces, axis=1), (SIDE, SIDE))


def correlate_cost(count):
    return pl.CostEstimate(
        flops=count * 12 * 2 * SIDE**3 * 2,
        bytes_accessed=count * CELLS * 10,
        transcendentals=count * CELLS * 3,
    )


def correlate_early(near, windows, tables):
    return pl.pallas_call(
        correlate_group,
        out_shape=jax.ShapeDtypeStruct((3, HALF, SIDE), f32),
        in_specs=[vectors] * 4,
        out_specs=vectors,
        compiler_params=pltpu.CompilerParams(vmem_limit_bytes=32 * 1024 * 1024),
        cost_estimate=correlate_cost(HALF),
    )(near, windows, *tables)


def correlate_late(live, ids, early, near, windows, tables):
    return pl.pallas_call(
        late_kernel,
        out_shape=jax.ShapeDtypeStruct((SIDE, SIDE), f32),
        in_specs=[scalars] + [vectors] * 6,
        out_specs=vectors,
        scratch_shapes=[pltpu.VMEM((3, HALF, SIDE), f32)],
        compiler_params=pltpu.CompilerParams(vmem_limit_bytes=32 * 1024 * 1024),
        cost_estimate=correlate_cost(HALF),
    )(live, ids, early, near, windows, *tables)


def collect_kernel(packed_ref, out_ref):
    packed = packed_ref[...].T
    base = (lax.axis_index("tiles") * lax.axis_size("grp") + lax.axis_index("grp")) * SIDE
    device = lax.broadcasted_iota(jnp.int32, (HALF, SIDE), 1)
    node = lax.broadcasted_iota(jnp.int32, (SIDE, SIDE), 0).astype(f32)
    sums = [jnp.zeros((SIDE, SIDE), f32), jnp.zeros((SIDE, SIDE), f32)]
    scale = 8.0 / SIDE
    for r, bit in enumerate(BITS):
        reach = 2 << bit
        side = (device >> (bit + 1)) & 1
        plain, ramp, edge, coord, chosen = (
            packed[2 * SLOTS + SLOTS * i + HALF * r :][:HALF] for i in range(5)
        )
        inverse = scale / plain
        own = [ramp * inverse, coord * inverse]
        other = []
        for shift, border in zip(own, (edge, chosen)):
            far = -shift - border * inverse * SIDE
            upper = pltpu.roll(far, SIDE - reach, 1)
            lower = pltpu.roll(far, reach, 1)
            other.append(jnp.where(side == 0, upper, lower))
        for h in range(2):
            local = packed[SLOTS * r + HALF * h :][:HALF] - base.astype(f32)
            values = [jnp.where(side == h, own[c], other[c]) for c in range(2)]
            for j in range(HALF):
                hit = node == local[j : j + 1]
                for c in range(2):
                    sums[c] = sums[c] + jnp.where(hit, values[c][j : j + 1], 0.0)
    ones = jnp.ones((8, SIDE), f32)
    for c in range(2):
        summed = lax.dot_general(
            ones,
            sums[c],
            (((1,), (1,)), ((), ())),
            precision=lax.Precision.HIGHEST,
            preferred_element_type=f32,
        )
        out_ref[c : c + 1] = summed[0:1]


def collect(packed):
    return pl.pallas_call(
        collect_kernel,
        out_shape=jax.ShapeDtypeStruct((2, SIDE), f32),
        in_specs=[pl.BlockSpec(memory_space=pltpu.VMEM)],
        out_specs=pl.BlockSpec(memory_space=pltpu.VMEM),
        compiler_params=pltpu.CompilerParams(vmem_limit_bytes=8 * 1024 * 1024),
    )(packed)


def swap(x, bit):
    pairs = [(i, i ^ (1 << bit)) for i in range(lax.axis_size("tiles"))]
    return lax.ppermute(x, "tiles", pairs)


def on_device(strips, edge_colour, patch_offsets, patch_live, node_ids):
    tables = [jnp.asarray(table) for table in fourier_tables()]
    corners = jnp.transpose(patch_offsets, (0, 1, 3, 2))
    held, send_early = hold(edge_colour, corners, strips)
    far_early = swap(send_early, BITS[0])
    far_late = swap(cut_late(edge_colour, corners, held), BITS[1])
    near_early, near_late = near_spectra(edge_colour, corners, held, *tables)
    early = correlate_early(near_early, far_early, tables)
    packed = correlate_late(patch_live, node_ids, early, near_late, far_late, tables)
    packed = packed.reshape(SIDE, 1, SIDE)
    gathered = lax.all_to_all(packed, ("tiles", "grp"), 0, 0, tiled=True)
    return collect(gathered.reshape(SIDE, SIDE))


def solution(mesh):
    placed = (
        P(("tiles", "grp"), None, None),
        P(("tiles", "grp"), None),
        P(("tiles", "grp"), None, None, None),
        P(("tiles", "grp"), None),
        P(("tiles", "grp"), None, None),
    )
    return jax.shard_map(
        on_device, mesh=mesh, in_specs=placed, out_specs=P(None, ("tiles", "grp")), check_vma=False
    )
```

```python
import functools
import math

import jax
import jax.numpy as jnp
import ml_dtypes
import numpy as np
from jax import lax
from jax.experimental import pallas as pl
from jax.experimental.pallas import tpu as pltpu
from jax.sharding import PartitionSpec as P

SIDE = 128
HALF = 8
SLOTS = 16
ROWS = 64
CELLS = SIDE * SIDE
BITS = (0, 5)

f32 = jnp.float32
bf16 = jnp.bfloat16


def fourier_tables():
    index = np.arange(SIDE)
    angle = (np.outer(index, index) % SIDE) * (2.0 * math.pi / SIDE)
    cosine, sine = np.cos(angle), np.sin(angle)

    def pieces(table):
        high = table.astype(ml_dtypes.bfloat16)
        low = (table - high.astype(np.float64)).astype(ml_dtypes.bfloat16)
        return high, low

    cos_high, cos_low = pieces(cosine)
    sin_high, sin_low = pieces(sine)
    first = np.block([[cos_high, sin_high], [cos_low, sin_low]])
    left_high = np.block([[cos_high, -sin_high], [sin_high, cos_high]])
    left_low = np.block([[cos_low, -sin_low], [sin_low, cos_low]])
    second = np.concatenate([left_high.T, left_high.T, left_low.T], axis=0)
    return first, second


def tile_side(bit):
    return (lax.axis_index("tiles") >> bit) & 1


def cut_windows(r, mine, colour_ref, corner_ref, held_ref):
    last = held_ref.shape[2] // SIDE - 1
    rows = lax.broadcasted_iota(jnp.int32, (SIDE, SIDE), 0)
    lanes = lax.broadcasted_iota(jnp.int32, (SIDE, SIDE), 1)
    colour = colour_ref[0, r]
    side = tile_side(BITS[r])
    start = HALF * side if mine else HALF - HALF * side
    for j in range(HALF):
        row = corner_ref[0, r, 0, start + j]
        col = corner_ref[0, r, 1, start + j]
        block = col >> 7
        shift = col - block * SIDE
        halves = []
        for b in (block, jnp.minimum(block + 1, last)):
            at = pl.ds(pl.multiple_of(b * SIDE, SIDE), SIDE)
            top = held_ref[colour, :SIDE, at].astype(f32)
            bottom = held_ref[colour, SIDE:, at].astype(f32)
            halves.append(jnp.where(rows >= row, top, bottom))
        yield jnp.where(lanes >= shift, *halves).astype(bf16)


def hold_kernel(
    colour_hbm,
    corner_hbm,
    strips_ref,
    held_ref,
    early_ref,
    late_ref,
    colour_ref,
    corner_ref,
    sems,
    small_sems,
):
    small = [
        pltpu.make_async_copy(colour_hbm, colour_ref, small_sems.at[0]),
        pltpu.make_async_copy(corner_hbm, corner_ref, small_sems.at[1]),
    ]
    large = []
    for i in range(strips_ref.shape[0]):
        for j in range(strips_ref.shape[1] // ROWS):
            rows = pl.ds(j * ROWS, ROWS)
            large.append(
                pltpu.make_async_copy(strips_ref.at[i, rows], held_ref.at[i, rows], sems.at[i, j])
            )
    for copy in small + large:
        copy.start()
    for copy in small + large:
        copy.wait()
    for r, send_ref in enumerate((early_ref, late_ref)):
        for j, window in enumerate(cut_windows(r, False, colour_ref, corner_ref, held_ref)):
            send_ref[j] = window


scalars = pl.BlockSpec(memory_space=pltpu.SMEM)
vectors = pl.BlockSpec(memory_space=pltpu.VMEM)
far_memory = pl.BlockSpec(memory_space=pltpu.HBM)


def cut_cost(bytes_accessed):
    return pl.CostEstimate(
        flops=HALF * CELLS * 8, bytes_accessed=bytes_accessed, transcendentals=0
    )


def hold(colour, corners, strips):
    return pl.pallas_call(
        hold_kernel,
        out_shape=(
            jax.ShapeDtypeStruct(strips.shape, bf16),
            jax.ShapeDtypeStruct((HALF, SIDE, SIDE), bf16),
            jax.ShapeDtypeStruct((HALF, SIDE, SIDE), bf16),
        ),
        in_specs=[far_memory] * 3,
        out_specs=(vectors,) * 3,
        scratch_shapes=[
            pltpu.SMEM(colour.shape, jnp.int32),
            pltpu.SMEM(corners.shape, jnp.int32),
            pltpu.SemaphoreType.DMA((2, strips.shape[1] // ROWS)),
            pltpu.SemaphoreType.DMA((2,)),
        ],
        compiler_params=pltpu.CompilerParams(vmem_limit_bytes=16 * 1024 * 1024),
        cost_estimate=cut_cost(2 * strips.size),
    )(*(pltpu.with_memory_space_constraint(x, pltpu.HBM) for x in (colour, corners, strips)))


def split(x):
    high = x.astype(bf16)
    return high, (x - high.astype(f32)).astype(bf16)


def matmul(a, b):
    return jnp.dot(a, b, preferred_element_type=f32)


def second_mul(high, low, second):
    return matmul(jnp.concatenate([high, low, high], axis=1), second)


def turned(x):
    blocks = []
    for i in range(x.shape[0] // SIDE):
        rows = x[i * SIDE : (i + 1) * SIDE]
        blocks.append(jnp.concatenate([rows[:, :SIDE].T, rows[:, SIDE:].T], axis=1))
    return jnp.concatenate(blocks, axis=0)


def forward(windows, first, second):
    rows = matmul(jnp.concatenate([windows, windows], axis=1), first)
    high, low = split(rows)
    return second_mul(turned(high), turned(low), second)


def near_kernel(colour_ref, corner_ref, held_ref, first_ref, second_ref, early_ref, late_ref):
    for r, out_ref in enumerate((early_ref, late_ref)):
        windows = jnp.concatenate(
            list(cut_windows(r, True, colour_ref, corner_ref, held_ref)), axis=0
        )
        out_ref[...] = forward(windows, first_ref[...], second_ref[...])


def near_spectra(colour, corners, held, first, second):
    shape = jax.ShapeDtypeStruct((HALF * SIDE, 2 * SIDE), f32)
    return pl.pallas_call(
        near_kernel,
        out_shape=(shape, shape),
        in_specs=[scalars, scalars] + [vectors] * 3,
        out_specs=(vectors, vectors),
        compiler_params=pltpu.CompilerParams(vmem_limit_bytes=32 * 1024 * 1024),
        cost_estimate=pl.CostEstimate(
            flops=SLOTS * 8 * 2 * SIDE**3 * 2, bytes_accessed=SLOTS * CELLS * 10, transcendentals=0
        ),
    )(colour, corners, held, first, second)


def patch_rows(x, p):
    return x[p * SIDE : (p + 1) * SIDE]


def down(x):
    return jnp.sum(x, axis=0, keepdims=True)


def across(rows):
    return jnp.sum(jnp.concatenate(rows, axis=0), axis=1, keepdims=True)


def correlate_group(near_ref, window_ref, first_ref, second_ref, sums_ref):
    far = forward(window_ref[...].reshape(HALF * SIDE, SIDE), first_ref[...], second_ref[...])
    crosses, sizes, size_rows = [], [], []
    for p in range(HALF):
        here, there = near_ref[p * SIDE : (p + 1) * SIDE, :], patch_rows(far, p)
        near_real, near_imag = here[:, :SIDE], here[:, SIDE:]
        far_real, far_imag = there[:, :SIDE], there[:, SIDE:]
        real = near_real * far_real + near_imag * far_imag
        imag = near_real * far_imag - near_imag * far_real
        size = jnp.sqrt(real * real + imag * imag)
        crosses.append((real, imag))
        sizes.append(size)
        size_rows.append(down(size))
    floors = across(size_rows) * (0.1 / CELLS) + 1e-6
    whites = []
    for p in range(HALF):
        scale = 1.0 / (sizes[p] + floors[p : p + 1])
        whites.append((crosses[p][0] * scale, crosses[p][1] * scale))
    spectra = []
    for q in range(HALF // 2):
        (a_real, a_imag), (b_real, b_imag) = whites[2 * q], whites[2 * q + 1]
        spectra.append(jnp.concatenate([a_real - b_imag, a_imag + b_real], axis=1))
    back = second_mul(*split(jnp.concatenate(spectra, axis=0)), second_ref[...])
    high, low = split(back)
    surfaces = second_mul(turned(high), turned(low), second_ref[...])
    patches = []
    for p in range(HALF):
        q, h = divmod(p, 2)
        patches.append(patch_rows(surfaces, q)[:, h * SIDE : (h + 1) * SIDE])
    mean = across([down(x) for x in patches]) * (1.0 / CELLS)
    square = across([down(x * x) for x in patches]) * (1.0 / CELLS)
    peak = jnp.max(
        jnp.concatenate([jnp.max(x, axis=0, keepdims=True) for x in patches], axis=0),
        axis=1,
        keepdims=True,
    )
    variance = jnp.maximum(square - mean * mean, 0.0)
    factor = (2.0 / CELLS) / jnp.sqrt(variance * (1.0 / CELLS**2) + 1e-6)
    row_index = lax.broadcasted_iota(jnp.int32, (SIDE, SIDE), 0)
    row_coord = (((row_index + SIDE // 2) & (SIDE - 1)) - SIDE // 2).astype(f32)
    for p, surface in enumerate(patches):
        weight = jnp.exp((surface - peak[p : p + 1]) * factor[p : p + 1])
        sums_ref[0, p : p + 1, :] = down(weight)
        sums_ref[1, p : p + 1, :] = down(weight * row_coord)
        sums_ref[2, p : p + 1, :] = weight[SIDE // 2 : SIDE // 2 + 1, :]


def late_kernel(
    live_ref, ids_ref, early_ref, near_ref, window_ref, first_ref, second_ref, out_ref, late_ref
):
    correlate_group(near_ref, window_ref, first_ref, second_ref, late_ref)
    terms = []
    for i in range(3):
        terms += [early_ref[i], late_ref[i]]
    terms.append(jnp.zeros((SIDE - 3 * SLOTS, SIDE), f32))
    flat = jnp.concatenate(terms, axis=0).T
    index = lax.broadcasted_iota(jnp.int32, (SIDE, SIDE), 0)
    coord = (((index + SIDE // 2) & (SIDE - 1)) - SIDE // 2).astype(f32)
    sums = down(flat)
    ramped = down(flat * coord)
    slot = lax.broadcasted_iota(jnp.int32, (1, SLOTS), 1)
    pieces = []
    for r in range(2):
        ids = jnp.where(slot < live_ref[0, r], ids_ref[0, r : r + 1, :], -1)
        pieces.append(ids.astype(f32))
    pieces += [sums[:, : 3 * SLOTS], ramped[:, :SLOTS], flat[SIDE // 2 : SIDE // 2 + 1, :SLOTS]]
    pieces.append(jnp.zeros((1, SIDE - 7 * SLOTS), f32))
    out_ref[...] = jnp.broadcast_to(jnp.concatenate(pieces, axis=1), (SIDE, SIDE))


def correlate_cost(count):
    return pl.CostEstimate(
        flops=count * 12 * 2 * SIDE**3 * 2,
        bytes_accessed=count * CELLS * 10,
        transcendentals=count * CELLS * 3,
    )


def correlate_early(near, windows, tables):
    return pl.pallas_call(
        correlate_group,
        out_shape=jax.ShapeDtypeStruct((3, HALF, SIDE), f32),
        in_specs=[vectors] * 4,
        out_specs=vectors,
        compiler_params=pltpu.CompilerParams(vmem_limit_bytes=32 * 1024 * 1024),
        cost_estimate=correlate_cost(HALF),
    )(near, windows, *tables)


def correlate_late(live, ids, early, near, windows, tables):
    return pl.pallas_call(
        late_kernel,
        out_shape=jax.ShapeDtypeStruct((SIDE, SIDE), f32),
        in_specs=[scalars] + [vectors] * 6,
        out_specs=vectors,
        scratch_shapes=[pltpu.VMEM((3, HALF, SIDE), f32)],
        compiler_params=pltpu.CompilerParams(vmem_limit_bytes=32 * 1024 * 1024),
        cost_estimate=correlate_cost(HALF),
    )(live, ids, early, near, windows, *tables)


def collect_kernel(packed_ref, out_ref):
    packed = packed_ref[...].T
    base = (lax.axis_index("tiles") * lax.axis_size("grp") + lax.axis_index("grp")) * SIDE
    device = lax.broadcasted_iota(jnp.int32, (HALF, SIDE), 1)
    node = lax.broadcasted_iota(jnp.int32, (SIDE, SIDE), 0).astype(f32)
    sums = [jnp.zeros((SIDE, SIDE), f32), jnp.zeros((SIDE, SIDE), f32)]
    scale = 8.0 / SIDE
    for r, bit in enumerate(BITS):
        reach = 2 << bit
        side = (device >> (bit + 1)) & 1
        plain, ramp, edge, coord, chosen = (
            packed[2 * SLOTS + SLOTS * i + HALF * r :][:HALF] for i in range(5)
        )
        inverse = scale / plain
        own = [ramp * inverse, coord * inverse]
        other = []
        for shift, border in zip(own, (edge, chosen)):
            far = -shift - border * inverse * SIDE
            upper = pltpu.roll(far, SIDE - reach, 1)
            lower = pltpu.roll(far, reach, 1)
            other.append(jnp.where(side == 0, upper, lower))
        for h in range(2):
            local = packed[SLOTS * r + HALF * h :][:HALF] - base.astype(f32)
            values = [jnp.where(side == h, own[c], other[c]) for c in range(2)]
            for j in range(HALF):
                hit = node == local[j : j + 1]
                for c in range(2):
                    sums[c] = sums[c] + jnp.where(hit, values[c][j : j + 1], 0.0)
    for c in range(2):
        out_ref[c : c + 1] = down(sums[c].T)


def collect(packed):
    return pl.pallas_call(
        collect_kernel,
        out_shape=jax.ShapeDtypeStruct((2, SIDE), f32),
        in_specs=[pl.BlockSpec(memory_space=pltpu.VMEM)],
        out_specs=pl.BlockSpec(memory_space=pltpu.VMEM),
        compiler_params=pltpu.CompilerParams(vmem_limit_bytes=8 * 1024 * 1024),
    )(packed)


def swap(x, bit):
    pairs = [(i, i ^ (1 << bit)) for i in range(lax.axis_size("tiles"))]
    return lax.ppermute(x, "tiles", pairs)


def on_device(strips, edge_colour, patch_offsets, patch_live, node_ids):
    tables = [jnp.asarray(table) for table in fourier_tables()]
    corners = jnp.transpose(patch_offsets, (0, 1, 3, 2))
    held, send_early, send_late = hold(edge_colour, corners, strips)
    far_early = swap(send_early, BITS[0])
    far_late = swap(send_late, BITS[1])
    near_early, near_late = near_spectra(edge_colour, corners, held, *tables)
    early = correlate_early(near_early, far_early, tables)
    packed = correlate_late(patch_live, node_ids, early, near_late, far_late, tables)
    packed = packed.reshape(SIDE, 1, SIDE)
    gathered = lax.all_to_all(packed, ("tiles", "grp"), 0, 0, tiled=True)
    return collect(gathered.reshape(SIDE, SIDE))


def solution(mesh):
    placed = (
        P(("tiles", "grp"), None, None),
        P(("tiles", "grp"), None),
        P(("tiles", "grp"), None, None, None),
        P(("tiles", "grp"), None),
        P(("tiles", "grp"), None, None),
    )
    return jax.shard_map(
        on_device, mesh=mesh, in_specs=placed, out_specs=P(None, ("tiles", "grp")), check_vma=False
    )
```

```python
import functools
import math

import jax
import jax.numpy as jnp
import ml_dtypes
import numpy as np
from jax import lax
from jax.experimental import pallas as pl
from jax.experimental.pallas import tpu as pltpu
from jax.sharding import PartitionSpec as P

SIDE = 128
HALF = 8
SLOTS = 16
ROWS = 64
CELLS = SIDE * SIDE
BITS = (0, 5)

f32 = jnp.float32
bf16 = jnp.bfloat16


def fourier_tables():
    index = np.arange(SIDE)
    angle = (np.outer(index, index) % SIDE) * (2.0 * math.pi / SIDE)
    cosine, sine = np.cos(angle), np.sin(angle)

    def pieces(table):
        high = table.astype(ml_dtypes.bfloat16)
        low = (table - high.astype(np.float64)).astype(ml_dtypes.bfloat16)
        return high, low

    cos_high, cos_low = pieces(cosine)
    sin_high, sin_low = pieces(sine)
    first = np.block([[cos_high, sin_high], [cos_low, sin_low]])
    left_high = np.block([[cos_high, -sin_high], [sin_high, cos_high]])
    left_low = np.block([[cos_low, -sin_low], [sin_low, cos_low]])
    second = np.concatenate([left_high.T, left_high.T, left_low.T], axis=0)
    return first, second


def tile_side(bit):
    return (lax.axis_index("tiles") >> bit) & 1


def cut_windows(r, mine, colour_ref, corner_ref, held_ref):
    last = held_ref.shape[2] // SIDE - 1
    rows = lax.broadcasted_iota(jnp.int32, (SIDE, SIDE), 0)
    lanes = lax.broadcasted_iota(jnp.int32, (SIDE, SIDE), 1)
    colour = colour_ref[0, r]
    side = tile_side(BITS[r])
    start = HALF * side if mine else HALF - HALF * side
    for j in range(HALF):
        row = corner_ref[0, r, 0, start + j]
        col = corner_ref[0, r, 1, start + j]
        block = col >> 7
        shift = col - block * SIDE
        halves = []
        for b in (block, jnp.minimum(block + 1, last)):
            at = pl.ds(pl.multiple_of(b * SIDE, SIDE), SIDE)
            top = held_ref[colour, :SIDE, at].astype(f32)
            bottom = held_ref[colour, SIDE:, at].astype(f32)
            halves.append(jnp.where(rows >= row, top, bottom))
        yield jnp.where(lanes >= shift, *halves).astype(bf16)


def hold_kernel(
    colour_hbm,
    corner_hbm,
    strips_ref,
    held_ref,
    early_ref,
    late_ref,
    colour_ref,
    corner_ref,
    sems,
    small_sems,
):
    small = [
        pltpu.make_async_copy(colour_hbm, colour_ref, small_sems.at[0]),
        pltpu.make_async_copy(corner_hbm, corner_ref, small_sems.at[1]),
    ]
    large = []
    for i in range(strips_ref.shape[0]):
        for j in range(strips_ref.shape[1] // ROWS):
            rows = pl.ds(j * ROWS, ROWS)
            large.append(
                pltpu.make_async_copy(strips_ref.at[i, rows], held_ref.at[i, rows], sems.at[i, j])
            )
    for copy in small + large:
        copy.start()
    for copy in small + large:
        copy.wait()
    for r, send_ref in enumerate((early_ref, late_ref)):
        for j, window in enumerate(cut_windows(r, False, colour_ref, corner_ref, held_ref)):
            send_ref[j] = window


scalars = pl.BlockSpec(memory_space=pltpu.SMEM)
vectors = pl.BlockSpec(memory_space=pltpu.VMEM)
far_memory = pl.BlockSpec(memory_space=pltpu.HBM)


def cut_cost(bytes_accessed):
    return pl.CostEstimate(
        flops=HALF * CELLS * 8, bytes_accessed=bytes_accessed, transcendentals=0
    )


def hold(colour, corners, strips):
    return pl.pallas_call(
        hold_kernel,
        out_shape=(
            jax.ShapeDtypeStruct(strips.shape, bf16),
            jax.ShapeDtypeStruct((HALF, SIDE, SIDE), bf16),
            jax.ShapeDtypeStruct((HALF, SIDE, SIDE), bf16),
        ),
        in_specs=[far_memory] * 3,
        out_specs=(vectors,) * 3,
        scratch_shapes=[
            pltpu.SMEM(colour.shape, jnp.int32),
            pltpu.SMEM(corners.shape, jnp.int32),
            pltpu.SemaphoreType.DMA((2, strips.shape[1] // ROWS)),
            pltpu.SemaphoreType.DMA((2,)),
        ],
        compiler_params=pltpu.CompilerParams(vmem_limit_bytes=16 * 1024 * 1024),
        cost_estimate=cut_cost(2 * strips.size),
    )(*(pltpu.with_memory_space_constraint(x, pltpu.HBM) for x in (colour, corners, strips)))


def split(x):
    high = x.astype(bf16)
    return high, (x - high.astype(f32)).astype(bf16)


def matmul(a, b):
    return jnp.dot(a, b, preferred_element_type=f32)


def second_mul(high, low, second):
    return matmul(jnp.concatenate([high, low, high], axis=1), second)


def turned(x):
    blocks = []
    for i in range(x.shape[0] // SIDE):
        rows = x[i * SIDE : (i + 1) * SIDE]
        blocks.append(jnp.concatenate([rows[:, :SIDE].T, rows[:, SIDE:].T], axis=1))
    return jnp.concatenate(blocks, axis=0)


def forward(windows, first, second):
    rows = matmul(jnp.concatenate([windows, windows], axis=1), first)
    high, low = split(rows)
    return second_mul(turned(high), turned(low), second)


def near_kernel(colour_ref, corner_ref, held_ref, first_ref, second_ref, early_ref, late_ref):
    for r, out_ref in enumerate((early_ref, late_ref)):
        windows = jnp.concatenate(
            list(cut_windows(r, True, colour_ref, corner_ref, held_ref)), axis=0
        )
        out_ref[...] = forward(windows, first_ref[...], second_ref[...])


def near_spectra(colour, corners, held, first, second):
    shape = jax.ShapeDtypeStruct((HALF * SIDE, 2 * SIDE), f32)
    return pl.pallas_call(
        near_kernel,
        out_shape=(shape, shape),
        in_specs=[scalars, scalars] + [vectors] * 3,
        out_specs=(vectors, vectors),
        compiler_params=pltpu.CompilerParams(vmem_limit_bytes=32 * 1024 * 1024),
        cost_estimate=pl.CostEstimate(
            flops=SLOTS * 8 * 2 * SIDE**3 * 2, bytes_accessed=SLOTS * CELLS * 10, transcendentals=0
        ),
    )(colour, corners, held, first, second)


def patch_rows(x, p):
    return x[p * SIDE : (p + 1) * SIDE]


def down(x):
    return jnp.sum(x, axis=0, keepdims=True)


def across(rows):
    return jnp.sum(jnp.concatenate(rows, axis=0), axis=1, keepdims=True)


def correlate_group(near_ref, window_ref, first_ref, second_ref, sums_ref):
    far = forward(window_ref[...].reshape(HALF * SIDE, SIDE), first_ref[...], second_ref[...])
    crosses, sizes, size_rows = [], [], []
    for p in range(HALF):
        here, there = near_ref[p * SIDE : (p + 1) * SIDE, :], patch_rows(far, p)
        near_real, near_imag = here[:, :SIDE], here[:, SIDE:]
        far_real, far_imag = there[:, :SIDE], there[:, SIDE:]
        real = near_real * far_real + near_imag * far_imag
        imag = near_real * far_imag - near_imag * far_real
        size = jnp.sqrt(real * real + imag * imag)
        crosses.append((real, imag))
        sizes.append(size)
        size_rows.append(down(size))
    floors = across(size_rows) * (0.1 / CELLS) + 1e-6
    whites, power_rows, centres = [], [], []
    for p in range(HALF):
        scale = 1.0 / (sizes[p] + floors[p : p + 1])
        white = (crosses[p][0] * scale, crosses[p][1] * scale)
        whites.append(white)
        weighted = sizes[p] * scale
        power_rows.append(down(weighted * weighted))
        centres.append(white[0][0:1, 0:1])
    centre = jnp.concatenate(centres, axis=0)
    variance = jnp.maximum(across(power_rows) - centre * centre, 0.0)
    factor = (2.0 / CELLS) / jnp.sqrt(variance * (1.0 / CELLS**2) + 1e-6)
    spectra = []
    for q in range(HALF // 2):
        (a_real, a_imag), (b_real, b_imag) = whites[2 * q], whites[2 * q + 1]
        spectra.append(jnp.concatenate([a_real - b_imag, a_imag + b_real], axis=1))
    back = second_mul(*split(jnp.concatenate(spectra, axis=0)), second_ref[...])
    high, low = split(back)
    surfaces = second_mul(turned(high), turned(low), second_ref[...])
    patches = []
    for p in range(HALF):
        q, h = divmod(p, 2)
        patches.append(patch_rows(surfaces, q)[:, h * SIDE : (h + 1) * SIDE])
    peak = jnp.max(
        jnp.concatenate([jnp.max(x, axis=0, keepdims=True) for x in patches], axis=0),
        axis=1,
        keepdims=True,
    )
    row_index = lax.broadcasted_iota(jnp.int32, (SIDE, SIDE), 0)
    row_coord = (((row_index + SIDE // 2) & (SIDE - 1)) - SIDE // 2).astype(f32)
    for p, surface in enumerate(patches):
        weight = jnp.exp((surface - peak[p : p + 1]) * factor[p : p + 1])
        sums_ref[0, p : p + 1, :] = down(weight)
        sums_ref[1, p : p + 1, :] = down(weight * row_coord)
        sums_ref[2, p : p + 1, :] = weight[SIDE // 2 : SIDE // 2 + 1, :]


def late_kernel(
    live_ref, ids_ref, early_ref, near_ref, window_ref, first_ref, second_ref, out_ref, late_ref
):
    correlate_group(near_ref, window_ref, first_ref, second_ref, late_ref)
    terms = []
    for i in range(3):
        terms += [early_ref[i], late_ref[i]]
    terms.append(jnp.zeros((SIDE - 3 * SLOTS, SIDE), f32))
    flat = jnp.concatenate(terms, axis=0).T
    index = lax.broadcasted_iota(jnp.int32, (SIDE, SIDE), 0)
    coord = (((index + SIDE // 2) & (SIDE - 1)) - SIDE // 2).astype(f32)
    sums = down(flat)
    ramped = down(flat * coord)
    slot = lax.broadcasted_iota(jnp.int32, (1, SLOTS), 1)
    pieces = []
    for r in range(2):
        ids = jnp.where(slot < live_ref[0, r], ids_ref[0, r : r + 1, :], -1)
        pieces.append(ids.astype(f32))
    pieces += [sums[:, : 3 * SLOTS], ramped[:, :SLOTS], flat[SIDE // 2 : SIDE // 2 + 1, :SLOTS]]
    pieces.append(jnp.zeros((1, SIDE - 7 * SLOTS), f32))
    out_ref[...] = jnp.broadcast_to(jnp.concatenate(pieces, axis=1), (SIDE, SIDE))


def correlate_cost(count):
    return pl.CostEstimate(
        flops=count * 12 * 2 * SIDE**3 * 2,
        bytes_accessed=count * CELLS * 10,
        transcendentals=count * CELLS * 3,
    )


def correlate_early(near, windows, tables):
    return pl.pallas_call(
        correlate_group,
        out_shape=jax.ShapeDtypeStruct((3, HALF, SIDE), f32),
        in_specs=[vectors] * 4,
        out_specs=vectors,
        compiler_params=pltpu.CompilerParams(vmem_limit_bytes=32 * 1024 * 1024),
        cost_estimate=correlate_cost(HALF),
    )(near, windows, *tables)


def correlate_late(live, ids, early, near, windows, tables):
    return pl.pallas_call(
        late_kernel,
        out_shape=jax.ShapeDtypeStruct((SIDE, SIDE), f32),
        in_specs=[scalars] + [vectors] * 6,
        out_specs=vectors,
        scratch_shapes=[pltpu.VMEM((3, HALF, SIDE), f32)],
        compiler_params=pltpu.CompilerParams(vmem_limit_bytes=32 * 1024 * 1024),
        cost_estimate=correlate_cost(HALF),
    )(live, ids, early, near, windows, *tables)


def collect_kernel(packed_ref, out_ref):
    packed = packed_ref[...].T
    base = (lax.axis_index("tiles") * lax.axis_size("grp") + lax.axis_index("grp")) * SIDE
    device = lax.broadcasted_iota(jnp.int32, (HALF, SIDE), 1)
    node = lax.broadcasted_iota(jnp.int32, (SIDE, SIDE), 0).astype(f32)
    sums = [jnp.zeros((SIDE, SIDE), f32), jnp.zeros((SIDE, SIDE), f32)]
    scale = 8.0 / SIDE
    for r, bit in enumerate(BITS):
        reach = 2 << bit
        side = (device >> (bit + 1)) & 1
        plain, ramp, edge, coord, chosen = (
            packed[2 * SLOTS + SLOTS * i + HALF * r :][:HALF] for i in range(5)
        )
        inverse = scale / plain
        own = [ramp * inverse, coord * inverse]
        other = []
        for shift, border in zip(own, (edge, chosen)):
            far = -shift - border * inverse * SIDE
            upper = pltpu.roll(far, SIDE - reach, 1)
            lower = pltpu.roll(far, reach, 1)
            other.append(jnp.where(side == 0, upper, lower))
        for h in range(2):
            local = packed[SLOTS * r + HALF * h :][:HALF] - base.astype(f32)
            values = [jnp.where(side == h, own[c], other[c]) for c in range(2)]
            for j in range(HALF):
                hit = node == local[j : j + 1]
                for c in range(2):
                    sums[c] = sums[c] + jnp.where(hit, values[c][j : j + 1], 0.0)
    for c in range(2):
        out_ref[c : c + 1] = down(sums[c].T)


def collect(packed):
    return pl.pallas_call(
        collect_kernel,
        out_shape=jax.ShapeDtypeStruct((2, SIDE), f32),
        in_specs=[pl.BlockSpec(memory_space=pltpu.VMEM)],
        out_specs=pl.BlockSpec(memory_space=pltpu.VMEM),
        compiler_params=pltpu.CompilerParams(vmem_limit_bytes=8 * 1024 * 1024),
    )(packed)


def swap(x, bit):
    pairs = [(i, i ^ (1 << bit)) for i in range(lax.axis_size("tiles"))]
    return lax.ppermute(x, "tiles", pairs)


def on_device(strips, edge_colour, patch_offsets, patch_live, node_ids):
    tables = [jnp.asarray(table) for table in fourier_tables()]
    corners = jnp.transpose(patch_offsets, (0, 1, 3, 2))
    held, send_early, send_late = hold(edge_colour, corners, strips)
    far_early = swap(send_early, BITS[0])
    far_late = swap(send_late, BITS[1])
    near_early, near_late = near_spectra(edge_colour, corners, held, *tables)
    early = correlate_early(near_early, far_early, tables)
    packed = correlate_late(patch_live, node_ids, early, near_late, far_late, tables)
    packed = packed.reshape(SIDE, 1, SIDE)
    gathered = lax.all_to_all(packed, ("tiles", "grp"), 0, 0, tiled=True)
    return collect(gathered.reshape(SIDE, SIDE))


def solution(mesh):
    placed = (
        P(("tiles", "grp"), None, None),
        P(("tiles", "grp"), None),
        P(("tiles", "grp"), None, None, None),
        P(("tiles", "grp"), None),
        P(("tiles", "grp"), None, None),
    )
    return jax.shard_map(
        on_device, mesh=mesh, in_specs=placed, out_specs=P(None, ("tiles", "grp")), check_vma=False
    )
```

```python
import functools
import math

import jax
import jax.numpy as jnp
import ml_dtypes
import numpy as np
from jax import lax
from jax.experimental import pallas as pl
from jax.experimental.pallas import tpu as pltpu
from jax.sharding import PartitionSpec as P

SIDE = 128
HALF = 8
SLOTS = 16
ROWS = 64
CELLS = SIDE * SIDE
BITS = (0, 5)

f32 = jnp.float32
bf16 = jnp.bfloat16


def fourier_tables():
    index = np.arange(SIDE)
    angle = (np.outer(index, index) % SIDE) * (2.0 * math.pi / SIDE)
    cosine, sine = np.cos(angle), np.sin(angle)

    def pieces(table):
        high = table.astype(ml_dtypes.bfloat16)
        low = (table - high.astype(np.float64)).astype(ml_dtypes.bfloat16)
        return high, low

    cos_high, cos_low = pieces(cosine)
    sin_high, sin_low = pieces(sine)
    first = np.block([[cos_high, sin_high], [cos_low, sin_low]])
    left_high = np.block([[cos_high, -sin_high], [sin_high, cos_high]])
    left_low = np.block([[cos_low, -sin_low], [sin_low, cos_low]])
    second = np.concatenate([left_high.T, left_high.T, left_low.T], axis=0)
    return first, second


def tile_side(bit):
    return (lax.axis_index("tiles") >> bit) & 1


def cut_windows(r, mine, colour_ref, corner_ref, held_ref):
    last = held_ref.shape[2] // SIDE - 1
    rows = lax.broadcasted_iota(jnp.int32, (SIDE, SIDE), 0)
    lanes = lax.broadcasted_iota(jnp.int32, (SIDE, SIDE), 1)
    colour = colour_ref[0, r]
    side = tile_side(BITS[r])
    start = HALF * side if mine else HALF - HALF * side
    for j in range(HALF):
        row = corner_ref[0, r, 0, start + j]
        col = corner_ref[0, r, 1, start + j]
        block = col >> 7
        shift = col - block * SIDE
        halves = []
        for b in (block, jnp.minimum(block + 1, last)):
            at = pl.ds(pl.multiple_of(b * SIDE, SIDE), SIDE)
            top = held_ref[colour, :SIDE, at].astype(f32)
            bottom = held_ref[colour, SIDE:, at].astype(f32)
            halves.append(jnp.where(rows >= row, top, bottom))
        yield jnp.where(lanes >= shift, *halves).astype(bf16)


def hold_kernel(
    colour_hbm,
    corner_hbm,
    strips_ref,
    held_ref,
    early_ref,
    late_ref,
    colour_ref,
    corner_ref,
    sems,
    small_sems,
):
    small = [
        pltpu.make_async_copy(colour_hbm, colour_ref, small_sems.at[0]),
        pltpu.make_async_copy(corner_hbm, corner_ref, small_sems.at[1]),
    ]
    large = []
    for i in range(strips_ref.shape[0]):
        for j in range(strips_ref.shape[1] // ROWS):
            rows = pl.ds(j * ROWS, ROWS)
            large.append(
                pltpu.make_async_copy(strips_ref.at[i, rows], held_ref.at[i, rows], sems.at[i, j])
            )
    for copy in small + large:
        copy.start()
    for copy in small + large:
        copy.wait()
    for r, send_ref in enumerate((early_ref, late_ref)):
        for j, window in enumerate(cut_windows(r, False, colour_ref, corner_ref, held_ref)):
            send_ref[j] = window


scalars = pl.BlockSpec(memory_space=pltpu.SMEM)
vectors = pl.BlockSpec(memory_space=pltpu.VMEM)
far_memory = pl.BlockSpec(memory_space=pltpu.HBM)


def cut_cost(bytes_accessed):
    return pl.CostEstimate(
        flops=HALF * CELLS * 8, bytes_accessed=bytes_accessed, transcendentals=0
    )


def hold(colour, corners, strips):
    return pl.pallas_call(
        hold_kernel,
        out_shape=(
            jax.ShapeDtypeStruct(strips.shape, bf16),
            jax.ShapeDtypeStruct((HALF, SIDE, SIDE), bf16),
            jax.ShapeDtypeStruct((HALF, SIDE, SIDE), bf16),
        ),
        in_specs=[far_memory] * 3,
        out_specs=(vectors,) * 3,
        scratch_shapes=[
            pltpu.SMEM(colour.shape, jnp.int32),
            pltpu.SMEM(corners.shape, jnp.int32),
            pltpu.SemaphoreType.DMA((2, strips.shape[1] // ROWS)),
            pltpu.SemaphoreType.DMA((2,)),
        ],
        compiler_params=pltpu.CompilerParams(vmem_limit_bytes=16 * 1024 * 1024),
        cost_estimate=cut_cost(2 * strips.size),
    )(*(pltpu.with_memory_space_constraint(x, pltpu.HBM) for x in (colour, corners, strips)))


def split(x):
    high = x.astype(bf16)
    return high, (x - high.astype(f32)).astype(bf16)


def matmul(a, b):
    return jnp.dot(a, b, preferred_element_type=f32)


def second_mul(high, low, second):
    return matmul(jnp.concatenate([high, low, high], axis=1), second)


def turned(x):
    blocks = []
    for i in range(x.shape[0] // SIDE):
        rows = x[i * SIDE : (i + 1) * SIDE]
        blocks.append(jnp.concatenate([rows[:, :SIDE].T, rows[:, SIDE:].T], axis=1))
    return jnp.concatenate(blocks, axis=0)


def forward(windows, first, second):
    rows = matmul(jnp.concatenate([windows, windows], axis=1), first)
    high, low = split(rows)
    return second_mul(turned(high), turned(low), second)


def near_kernel(colour_ref, corner_ref, held_ref, first_ref, second_ref, early_ref, late_ref):
    for r, out_ref in enumerate((early_ref, late_ref)):
        windows = jnp.concatenate(
            list(cut_windows(r, True, colour_ref, corner_ref, held_ref)), axis=0
        )
        out_ref[...] = forward(windows, first_ref[...], second_ref[...])


def near_spectra(colour, corners, held, first, second):
    shape = jax.ShapeDtypeStruct((HALF * SIDE, 2 * SIDE), f32)
    return pl.pallas_call(
        near_kernel,
        out_shape=(shape, shape),
        in_specs=[scalars, scalars] + [vectors] * 3,
        out_specs=(vectors, vectors),
        compiler_params=pltpu.CompilerParams(vmem_limit_bytes=32 * 1024 * 1024),
        cost_estimate=pl.CostEstimate(
            flops=SLOTS * 8 * 2 * SIDE**3 * 2, bytes_accessed=SLOTS * CELLS * 10, transcendentals=0
        ),
    )(colour, corners, held, first, second)


def patch_rows(x, p):
    return x[p * SIDE : (p + 1) * SIDE]


def down(x):
    return jnp.sum(x, axis=0, keepdims=True)


def across(rows):
    return jnp.sum(jnp.concatenate(rows, axis=0), axis=1, keepdims=True)


def correlate_group(near_ref, window_ref, first_ref, second_ref, sums_ref):
    far = forward(window_ref[...].reshape(HALF * SIDE, SIDE), first_ref[...], second_ref[...])
    crosses, sizes, size_rows = [], [], []
    for p in range(HALF):
        here, there = near_ref[p * SIDE : (p + 1) * SIDE, :], patch_rows(far, p)
        near_real, near_imag = here[:, :SIDE], here[:, SIDE:]
        far_real, far_imag = there[:, :SIDE], there[:, SIDE:]
        real = near_real * far_real + near_imag * far_imag
        imag = near_real * far_imag - near_imag * far_real
        size = jnp.sqrt(real * real + imag * imag)
        crosses.append((real, imag))
        sizes.append(size)
        size_rows.append(down(size))
    floors = across(size_rows) * (0.1 / CELLS) + 1e-6
    whites = []
    for p in range(HALF):
        scale = 1.0 / (sizes[p] + floors[p : p + 1])
        whites.append((crosses[p][0] * scale, crosses[p][1] * scale))
    spectra = []
    for q in range(HALF // 2):
        (a_real, a_imag), (b_real, b_imag) = whites[2 * q], whites[2 * q + 1]
        spectra.append(jnp.concatenate([a_real - b_imag, a_imag + b_real], axis=1))
    back = second_mul(*split(jnp.concatenate(spectra, axis=0)), second_ref[...])
    high, low = split(back)
    surfaces = second_mul(turned(high), turned(low), second_ref[...])
    patches = []
    for p in range(HALF):
        q, h = divmod(p, 2)
        patches.append(patch_rows(surfaces, q)[:, h * SIDE : (h + 1) * SIDE])
    mean = across([down(x) for x in patches]) * (1.0 / CELLS)
    square = across([down(x * x) for x in patches]) * (1.0 / CELLS)
    peak = jnp.max(
        jnp.concatenate([jnp.max(x, axis=0, keepdims=True) for x in patches], axis=0),
        axis=1,
        keepdims=True,
    )
    variance = jnp.maximum(square - mean * mean, 0.0)
    factor = (2.0 / CELLS) / jnp.sqrt(variance * (1.0 / CELLS**2) + 1e-6)
    row_index = lax.broadcasted_iota(jnp.int32, (SIDE, SIDE), 0)
    row_coord = (((row_index + SIDE // 2) & (SIDE - 1)) - SIDE // 2).astype(f32)
    for p, surface in enumerate(patches):
        weight = jnp.exp((surface - peak[p : p + 1]) * factor[p : p + 1])
        sums_ref[0, p : p + 1, :] = down(weight)
        sums_ref[1, p : p + 1, :] = down(weight * row_coord)
        sums_ref[2, p : p + 1, :] = weight[SIDE // 2 : SIDE // 2 + 1, :]


def late_kernel(
    live_ref, ids_ref, early_ref, near_ref, window_ref, first_ref, second_ref, out_ref, late_ref
):
    correlate_group(near_ref, window_ref, first_ref, second_ref, late_ref)
    terms = []
    for i in range(3):
        terms += [late_ref[i], early_ref[i]]
    terms.append(jnp.zeros((SIDE - 3 * SLOTS, SIDE), f32))
    flat = jnp.concatenate(terms, axis=0).T
    index = lax.broadcasted_iota(jnp.int32, (SIDE, SIDE), 0)
    coord = (((index + SIDE // 2) & (SIDE - 1)) - SIDE // 2).astype(f32)
    sums = down(flat)
    ramped = down(flat * coord)
    slot = lax.broadcasted_iota(jnp.int32, (1, SLOTS), 1)
    pieces = []
    for r in range(2):
        ids = jnp.where(slot < live_ref[0, r], ids_ref[0, r : r + 1, :], -1)
        pieces.append(ids.astype(f32))
    pieces += [sums[:, : 3 * SLOTS], ramped[:, :SLOTS], flat[SIDE // 2 : SIDE // 2 + 1, :SLOTS]]
    pieces.append(jnp.zeros((1, SIDE - 7 * SLOTS), f32))
    out_ref[...] = jnp.broadcast_to(jnp.concatenate(pieces, axis=1), (SIDE, SIDE))


def correlate_cost(count):
    return pl.CostEstimate(
        flops=count * 12 * 2 * SIDE**3 * 2,
        bytes_accessed=count * CELLS * 10,
        transcendentals=count * CELLS * 3,
    )


def correlate_early(near, windows, tables):
    return pl.pallas_call(
        correlate_group,
        out_shape=jax.ShapeDtypeStruct((3, HALF, SIDE), f32),
        in_specs=[vectors] * 4,
        out_specs=vectors,
        compiler_params=pltpu.CompilerParams(vmem_limit_bytes=32 * 1024 * 1024),
        cost_estimate=correlate_cost(HALF),
    )(near, windows, *tables)


def correlate_late(live, ids, early, near, windows, tables):
    return pl.pallas_call(
        late_kernel,
        out_shape=jax.ShapeDtypeStruct((SIDE, SIDE), f32),
        in_specs=[scalars] + [vectors] * 6,
        out_specs=vectors,
        scratch_shapes=[pltpu.VMEM((3, HALF, SIDE), f32)],
        compiler_params=pltpu.CompilerParams(vmem_limit_bytes=32 * 1024 * 1024),
        cost_estimate=correlate_cost(HALF),
    )(live, ids, early, near, windows, *tables)


def collect_kernel(packed_ref, out_ref):
    packed = packed_ref[...].T
    base = (lax.axis_index("tiles") * lax.axis_size("grp") + lax.axis_index("grp")) * SIDE
    device = lax.broadcasted_iota(jnp.int32, (HALF, SIDE), 1)
    node = lax.broadcasted_iota(jnp.int32, (SIDE, SIDE), 0).astype(f32)
    sums = [jnp.zeros((SIDE, SIDE), f32), jnp.zeros((SIDE, SIDE), f32)]
    scale = 8.0 / SIDE
    for r, bit in enumerate(BITS):
        reach = 2 << bit
        side = (device >> (bit + 1)) & 1
        plain, ramp, edge, coord, chosen = (
            packed[2 * SLOTS + SLOTS * i + HALF * r :][:HALF] for i in range(5)
        )
        inverse = scale / plain
        own = [ramp * inverse, coord * inverse]
        other = []
        for shift, border in zip(own, (edge, chosen)):
            far = -shift - border * inverse * SIDE
            upper = pltpu.roll(far, SIDE - reach, 1)
            lower = pltpu.roll(far, reach, 1)
            other.append(jnp.where(side == 0, upper, lower))
        for h in range(2):
            local = packed[SLOTS * r + HALF * h :][:HALF] - base.astype(f32)
            values = [jnp.where(side == h, own[c], other[c]) for c in range(2)]
            for j in range(HALF):
                hit = node == local[j : j + 1]
                for c in range(2):
                    sums[c] = sums[c] + jnp.where(hit, values[c][j : j + 1], 0.0)
    for c in range(2):
        out_ref[c : c + 1] = down(sums[c].T)


def collect(packed):
    return pl.pallas_call(
        collect_kernel,
        out_shape=jax.ShapeDtypeStruct((2, SIDE), f32),
        in_specs=[pl.BlockSpec(memory_space=pltpu.VMEM)],
        out_specs=pl.BlockSpec(memory_space=pltpu.VMEM),
        compiler_params=pltpu.CompilerParams(vmem_limit_bytes=8 * 1024 * 1024),
    )(packed)


def swap(x, bit):
    pairs = [(i, i ^ (1 << bit)) for i in range(lax.axis_size("tiles"))]
    return lax.ppermute(x, "tiles", pairs)


def on_device(strips, edge_colour, patch_offsets, patch_live, node_ids):
    tables = [jnp.asarray(table) for table in fourier_tables()]
    corners = jnp.transpose(patch_offsets, (0, 1, 3, 2))
    held, send_early, send_late = hold(edge_colour, corners, strips)
    far_late = swap(send_late, BITS[1])
    far_early = swap(send_early, BITS[0])
    near_early, near_late = near_spectra(edge_colour, corners, held, *tables)
    early = correlate_early(near_late, far_late, tables)
    packed = correlate_late(patch_live, node_ids, early, near_early, far_early, tables)
    packed = packed.reshape(SIDE, 1, SIDE)
    gathered = lax.all_to_all(packed, ("tiles", "grp"), 0, 0, tiled=True)
    return collect(gathered.reshape(SIDE, SIDE))


def solution(mesh):
    placed = (
        P(("tiles", "grp"), None, None),
        P(("tiles", "grp"), None),
        P(("tiles", "grp"), None, None, None),
        P(("tiles", "grp"), None),
        P(("tiles", "grp"), None, None),
    )
    return jax.shard_map(
        on_device, mesh=mesh, in_specs=placed, out_specs=P(None, ("tiles", "grp")), check_vma=False
    )
```

```python
import functools
import math

import jax
import jax.numpy as jnp
import ml_dtypes
import numpy as np
from jax import lax
from jax.experimental import pallas as pl
from jax.experimental.pallas import tpu as pltpu
from jax.sharding import PartitionSpec as P

SIDE = 128
HALF = 8
SLOTS = 16
ROWS = 64
CELLS = SIDE * SIDE
BITS = (0, 5)

f32 = jnp.float32
bf16 = jnp.bfloat16


def fourier_tables():
    index = np.arange(SIDE)
    angle = (np.outer(index, index) % SIDE) * (2.0 * math.pi / SIDE)
    cosine, sine = np.cos(angle), np.sin(angle)

    def pieces(table):
        high = table.astype(ml_dtypes.bfloat16)
        low = (table - high.astype(np.float64)).astype(ml_dtypes.bfloat16)
        return high, low

    cos_high, cos_low = pieces(cosine)
    sin_high, sin_low = pieces(sine)
    first = np.block([[cos_high, sin_high], [cos_low, sin_low]])
    left_high = np.block([[cos_high, -sin_high], [sin_high, cos_high]])
    left_low = np.block([[cos_low, -sin_low], [sin_low, cos_low]])
    second = np.concatenate([left_high.T, left_high.T, left_low.T], axis=0)
    return first, second


def tile_side(bit):
    return (lax.axis_index("tiles") >> bit) & 1


def cut_windows(r, mine, colour_ref, corner_ref, held_ref):
    last = held_ref.shape[2] // SIDE - 1
    rows = lax.broadcasted_iota(jnp.int32, (SIDE, SIDE), 0)
    lanes = lax.broadcasted_iota(jnp.int32, (SIDE, SIDE), 1)
    colour = colour_ref[0, r]
    side = tile_side(BITS[r])
    start = HALF * side if mine else HALF - HALF * side
    for j in range(HALF):
        row = corner_ref[0, r, 0, start + j]
        col = corner_ref[0, r, 1, start + j]
        block = col >> 7
        shift = col - block * SIDE
        halves = []
        for b in (block, jnp.minimum(block + 1, last)):
            at = pl.ds(pl.multiple_of(b * SIDE, SIDE), SIDE)
            top = held_ref[colour, :SIDE, at]
            bottom = held_ref[colour, SIDE:, at]
            halves.append(jnp.where(rows >= row, top, bottom))
        yield jnp.where(lanes >= shift, *halves)


def hold_kernel(
    colour_hbm,
    corner_hbm,
    strips_ref,
    held_ref,
    early_ref,
    late_ref,
    colour_ref,
    corner_ref,
    sems,
    small_sems,
):
    small = [
        pltpu.make_async_copy(colour_hbm, colour_ref, small_sems.at[0]),
        pltpu.make_async_copy(corner_hbm, corner_ref, small_sems.at[1]),
    ]
    large = []
    for i in range(strips_ref.shape[0]):
        for j in range(strips_ref.shape[1] // ROWS):
            rows = pl.ds(j * ROWS, ROWS)
            large.append(
                pltpu.make_async_copy(strips_ref.at[i, rows], held_ref.at[i, rows], sems.at[i, j])
            )
    for copy in small + large:
        copy.start()
    for copy in small + large:
        copy.wait()
    for r, send_ref in enumerate((early_ref, late_ref)):
        for j, window in enumerate(cut_windows(r, False, colour_ref, corner_ref, held_ref)):
            send_ref[j] = window


scalars = pl.BlockSpec(memory_space=pltpu.SMEM)
vectors = pl.BlockSpec(memory_space=pltpu.VMEM)
far_memory = pl.BlockSpec(memory_space=pltpu.HBM)


def cut_cost(bytes_accessed):
    return pl.CostEstimate(
        flops=HALF * CELLS * 8, bytes_accessed=bytes_accessed, transcendentals=0
    )


def hold(colour, corners, strips):
    return pl.pallas_call(
        hold_kernel,
        out_shape=(
            jax.ShapeDtypeStruct(strips.shape, bf16),
            jax.ShapeDtypeStruct((HALF, SIDE, SIDE), bf16),
            jax.ShapeDtypeStruct((HALF, SIDE, SIDE), bf16),
        ),
        in_specs=[far_memory] * 3,
        out_specs=(vectors,) * 3,
        scratch_shapes=[
            pltpu.SMEM(colour.shape, jnp.int32),
            pltpu.SMEM(corners.shape, jnp.int32),
            pltpu.SemaphoreType.DMA((2, strips.shape[1] // ROWS)),
            pltpu.SemaphoreType.DMA((2,)),
        ],
        compiler_params=pltpu.CompilerParams(vmem_limit_bytes=16 * 1024 * 1024),
        cost_estimate=cut_cost(2 * strips.size),
    )(*(pltpu.with_memory_space_constraint(x, pltpu.HBM) for x in (colour, corners, strips)))


def split(x):
    high = x.astype(bf16)
    return high, (x - high.astype(f32)).astype(bf16)


def matmul(a, b):
    return jnp.dot(a, b, preferred_element_type=f32)


def second_mul(high, low, second):
    return matmul(jnp.concatenate([high, low, high], axis=1), second)


def turned(x):
    blocks = []
    for i in range(x.shape[0] // SIDE):
        rows = x[i * SIDE : (i + 1) * SIDE]
        blocks.append(jnp.concatenate([rows[:, :SIDE].T, rows[:, SIDE:].T], axis=1))
    return jnp.concatenate(blocks, axis=0)


def forward(windows, first, second):
    rows = matmul(jnp.concatenate([windows, windows], axis=1), first)
    high, low = split(rows)
    return second_mul(turned(high), turned(low), second)


def near_kernel(colour_ref, corner_ref, held_ref, first_ref, second_ref, early_ref, late_ref):
    for r, out_ref in enumerate((early_ref, late_ref)):
        windows = jnp.concatenate(
            list(cut_windows(r, True, colour_ref, corner_ref, held_ref)), axis=0
        )
        out_ref[...] = forward(windows, first_ref[...], second_ref[...])


def near_spectra(colour, corners, held, first, second):
    shape = jax.ShapeDtypeStruct((HALF * SIDE, 2 * SIDE), f32)
    return pl.pallas_call(
        near_kernel,
        out_shape=(shape, shape),
        in_specs=[scalars, scalars] + [vectors] * 3,
        out_specs=(vectors, vectors),
        compiler_params=pltpu.CompilerParams(vmem_limit_bytes=32 * 1024 * 1024),
        cost_estimate=pl.CostEstimate(
            flops=SLOTS * 8 * 2 * SIDE**3 * 2, bytes_accessed=SLOTS * CELLS * 10, transcendentals=0
        ),
    )(colour, corners, held, first, second)


def patch_rows(x, p):
    return x[p * SIDE : (p + 1) * SIDE]


def down(x):
    return jnp.sum(x, axis=0, keepdims=True)


def across(rows):
    return jnp.sum(jnp.concatenate(rows, axis=0), axis=1, keepdims=True)


def correlate_group(near_ref, window_ref, first_ref, second_ref, sums_ref):
    far = forward(window_ref[...].reshape(HALF * SIDE, SIDE), first_ref[...], second_ref[...])
    crosses, sizes, size_rows = [], [], []
    for p in range(HALF):
        here, there = near_ref[p * SIDE : (p + 1) * SIDE, :], patch_rows(far, p)
        near_real, near_imag = here[:, :SIDE], here[:, SIDE:]
        far_real, far_imag = there[:, :SIDE], there[:, SIDE:]
        real = near_real * far_real + near_imag * far_imag
        imag = near_real * far_imag - near_imag * far_real
        size = jnp.sqrt(real * real + imag * imag)
        crosses.append((real, imag))
        sizes.append(size)
        size_rows.append(down(size))
    floors = across(size_rows) * (0.1 / CELLS) + 1e-6
    whites = []
    for p in range(HALF):
        scale = 1.0 / (sizes[p] + floors[p : p + 1])
        whites.append((crosses[p][0] * scale, crosses[p][1] * scale))
    spectra = []
    for q in range(HALF // 2):
        (a_real, a_imag), (b_real, b_imag) = whites[2 * q], whites[2 * q + 1]
        spectra.append(jnp.concatenate([a_real - b_imag, a_imag + b_real], axis=1))
    back = second_mul(*split(jnp.concatenate(spectra, axis=0)), second_ref[...])
    high, low = split(back)
    surfaces = second_mul(turned(high), turned(low), second_ref[...])
    patches = []
    for p in range(HALF):
        q, h = divmod(p, 2)
        patches.append(patch_rows(surfaces, q)[:, h * SIDE : (h + 1) * SIDE])
    mean = across([down(x) for x in patches]) * (1.0 / CELLS)
    square = across([down(x * x) for x in patches]) * (1.0 / CELLS)
    peak = jnp.max(
        jnp.concatenate([jnp.max(x, axis=0, keepdims=True) for x in patches], axis=0),
        axis=1,
        keepdims=True,
    )
    variance = jnp.maximum(square - mean * mean, 0.0)
    factor = (2.0 / CELLS) / jnp.sqrt(variance * (1.0 / CELLS**2) + 1e-6)
    row_index = lax.broadcasted_iota(jnp.int32, (SIDE, SIDE), 0)
    row_coord = (((row_index + SIDE // 2) & (SIDE - 1)) - SIDE // 2).astype(f32)
    for p, surface in enumerate(patches):
        weight = jnp.exp((surface - peak[p : p + 1]) * factor[p : p + 1])
        sums_ref[0, p : p + 1, :] = down(weight)
        sums_ref[1, p : p + 1, :] = down(weight * row_coord)
        sums_ref[2, p : p + 1, :] = weight[SIDE // 2 : SIDE // 2 + 1, :]


def late_kernel(
    live_ref, ids_ref, early_ref, near_ref, window_ref, first_ref, second_ref, out_ref, late_ref
):
    correlate_group(near_ref, window_ref, first_ref, second_ref, late_ref)
    terms = []
    for i in range(3):
        terms += [early_ref[i], late_ref[i]]
    terms.append(jnp.zeros((SIDE - 3 * SLOTS, SIDE), f32))
    flat = jnp.concatenate(terms, axis=0).T
    index = lax.broadcasted_iota(jnp.int32, (SIDE, SIDE), 0)
    coord = (((index + SIDE // 2) & (SIDE - 1)) - SIDE // 2).astype(f32)
    sums = down(flat)
    ramped = down(flat * coord)
    slot = lax.broadcasted_iota(jnp.int32, (1, SLOTS), 1)
    pieces = []
    for r in range(2):
        ids = jnp.where(slot < live_ref[0, r], ids_ref[0, r : r + 1, :], -1)
        pieces.append(ids.astype(f32))
    pieces += [sums[:, : 3 * SLOTS], ramped[:, :SLOTS], flat[SIDE // 2 : SIDE // 2 + 1, :SLOTS]]
    pieces.append(jnp.zeros((1, SIDE - 7 * SLOTS), f32))
    out_ref[...] = jnp.broadcast_to(jnp.concatenate(pieces, axis=1), (SIDE, SIDE))


def correlate_cost(count):
    return pl.CostEstimate(
        flops=count * 12 * 2 * SIDE**3 * 2,
        bytes_accessed=count * CELLS * 10,
        transcendentals=count * CELLS * 3,
    )


def correlate_early(near, windows, tables):
    return pl.pallas_call(
        correlate_group,
        out_shape=jax.ShapeDtypeStruct((3, HALF, SIDE), f32),
        in_specs=[vectors] * 4,
        out_specs=vectors,
        compiler_params=pltpu.CompilerParams(vmem_limit_bytes=32 * 1024 * 1024),
        cost_estimate=correlate_cost(HALF),
    )(near, windows, *tables)


def correlate_late(live, ids, early, near, windows, tables):
    return pl.pallas_call(
        late_kernel,
        out_shape=jax.ShapeDtypeStruct((SIDE, SIDE), f32),
        in_specs=[scalars] + [vectors] * 6,
        out_specs=vectors,
        scratch_shapes=[pltpu.VMEM((3, HALF, SIDE), f32)],
        compiler_params=pltpu.CompilerParams(vmem_limit_bytes=32 * 1024 * 1024),
        cost_estimate=correlate_cost(HALF),
    )(live, ids, early, near, windows, *tables)


def collect_kernel(packed_ref, out_ref):
    packed = packed_ref[...].T
    base = (lax.axis_index("tiles") * lax.axis_size("grp") + lax.axis_index("grp")) * SIDE
    device = lax.broadcasted_iota(jnp.int32, (HALF, SIDE), 1)
    node = lax.broadcasted_iota(jnp.int32, (SIDE, SIDE), 0).astype(f32)
    sums = [jnp.zeros((SIDE, SIDE), f32), jnp.zeros((SIDE, SIDE), f32)]
    scale = 8.0 / SIDE
    for r, bit in enumerate(BITS):
        reach = 2 << bit
        side = (device >> (bit + 1)) & 1
        plain, ramp, edge, coord, chosen = (
            packed[2 * SLOTS + SLOTS * i + HALF * r :][:HALF] for i in range(5)
        )
        inverse = scale / plain
        own = [ramp * inverse, coord * inverse]
        other = []
        for shift, border in zip(own, (edge, chosen)):
            far = -shift - border * inverse * SIDE
            upper = pltpu.roll(far, SIDE - reach, 1)
            lower = pltpu.roll(far, reach, 1)
            other.append(jnp.where(side == 0, upper, lower))
        for h in range(2):
            local = packed[SLOTS * r + HALF * h :][:HALF] - base.astype(f32)
            values = [jnp.where(side == h, own[c], other[c]) for c in range(2)]
            for j in range(HALF):
                hit = node == local[j : j + 1]
                for c in range(2):
                    sums[c] = sums[c] + jnp.where(hit, values[c][j : j + 1], 0.0)
    for c in range(2):
        out_ref[c : c + 1] = down(sums[c].T)


def collect(packed):
    return pl.pallas_call(
        collect_kernel,
        out_shape=jax.ShapeDtypeStruct((2, SIDE), f32),
        in_specs=[pl.BlockSpec(memory_space=pltpu.VMEM)],
        out_specs=pl.BlockSpec(memory_space=pltpu.VMEM),
        compiler_params=pltpu.CompilerParams(vmem_limit_bytes=8 * 1024 * 1024),
    )(packed)


def swap(x, bit):
    pairs = [(i, i ^ (1 << bit)) for i in range(lax.axis_size("tiles"))]
    return lax.ppermute(x, "tiles", pairs)


def on_device(strips, edge_colour, patch_offsets, patch_live, node_ids):
    tables = [jnp.asarray(table) for table in fourier_tables()]
    corners = jnp.transpose(patch_offsets, (0, 1, 3, 2))
    held, send_early, send_late = hold(edge_colour, corners, strips)
    far_early = swap(send_early, BITS[0])
    far_late = swap(send_late, BITS[1])
    near_early, near_late = near_spectra(edge_colour, corners, held, *tables)
    early = correlate_early(near_early, far_early, tables)
    packed = correlate_late(patch_live, node_ids, early, near_late, far_late, tables)
    packed = packed.reshape(SIDE, 1, SIDE)
    gathered = lax.all_to_all(packed, ("tiles", "grp"), 0, 0, tiled=True)
    return collect(gathered.reshape(SIDE, SIDE))


def solution(mesh):
    placed = (
        P(("tiles", "grp"), None, None),
        P(("tiles", "grp"), None),
        P(("tiles", "grp"), None, None, None),
        P(("tiles", "grp"), None),
        P(("tiles", "grp"), None, None),
    )
    return jax.shard_map(
        on_device, mesh=mesh, in_specs=placed, out_specs=P(None, ("tiles", "grp")), check_vma=False
    )
```
